32 devices in a mesh: crop: 4 (over x, core), row: 8 (over z, y).
Axes of the slice: x: 2, y: 2, z: 4, core: 2. Of those that a mesh axis runs over, the one named last changes fastest.
Arguments:
- pair: bfloat16 [64, 16, 128], P(('crop', 'row')), parts along dimension 0, may hold values from -6 to 6
- out_grad: bfloat16 [64, 16, 128], P('crop', 'row'), parts along dimension 0, may hold values from -6 to 6
- w_qkvg: bfloat16 [128, 512], replicated, may hold values from -0.5 to 0.5
- w_out: bfloat16 [128, 128], replicated, may hold values from -0.5 to 0.5
- w_bias: bfloat16 [128, 4], replicated, may hold values from -32 to 32
- gain: float32 [128], replicated, may hold values from 0.1 to 1.9
Outputs:
- d_pair: bfloat16 [64, 16, 128], P(('crop', 'row')), parts along dimension 0
- d_qkvg: float32 [512, 512], P('crop'), parts along dimension 0
- d_wout: float32 [512, 128], P('crop'), parts along dimension 0
- d_wbias: float32 [512, 4], P('crop'), parts along dimension 0
- d_gain: float32 [512], P('crop'), parts along dimension 0
The draws below stay inside these ranges and needn't reach their ends.
There are 4 independent parts, one for each index of `crop`. The reference program is written for one: setup_inputs(seed, part) draws one part's arguments, and reference() takes and returns one part's arrays. A program takes and returns all parts, laid end to end along the dimension named above; an argument that names none is the same for every part. Nothing has to cross between parts.
All inputs are finite; a program needn't handle non-finite values.
Results may differ from the reference program's by a relative error of at most 0.014.
The reference program's roundings to bfloat16 on the way count: a program that leaves them out, or rounds other values in their place, can miss the bound.
Values may be sent and summed in bfloat16 or wider, within the bound.
A program may use at most 64 MiB of HBM per device.

```python
import jax
import jax.numpy as jnp
from jax import lax

C = 128
H = 4
DH = 32
N = 16


def draw_w_bias(key, part):
    base = jax.random.normal(key, (C, H), jnp.float32)
    weights = base * 1.5 * C ** (-0.5)
    return jnp.clip(weights, -32.0, 32.0).astype(jnp.bfloat16)


def block_scale(own_key, shape, split, low, largest):
    def one(position, shards_of):
        steps = jax.random.uniform(jax.random.fold_in(jax.random.fold_in(own_key, 6), position), (shards_of,), jnp.float32, low / len(split), largest / len(split))
        return jnp.repeat(jnp.exp(steps), shape[position] // shards_of).reshape((-1,) + (1,) * (len(shape) - position - 1))

    level = one(*split[0])
    for cut in split[1:]:
        level = level * one(*cut)
    return level


def scatter_about(own_key, extent, scale, reach, pieces=(), held_as=jnp.bfloat16):
    result = jax.random.normal(own_key, extent, jnp.float32) * scale
    if len(pieces) > 0:
        result = block_scale(own_key, extent, pieces, -0.22, 0.18) * result
    return jnp.clip(result, min=-reach, max=reach).astype(held_as)


def setup_inputs(seed: int = 0, part: int = 0) -> dict:
    key_list = jax.random.split(jax.random.key(seed), 7)
    part_splits = jax.random.split(jax.random.fold_in(key_list[6], part), 7)
    return {
        "pair": scatter_about(part_splits[0], (N, N, C), 1.0, 6.0, ((0, 8),)),
        "out_grad": scatter_about(part_splits[1], (N, N, C), 1.0, 6.0, ((1, 8),)),
        "w_qkvg": scatter_about(key_list[2], (C, 4 * C), C ** -0.5, 0.5),
        "w_out": scatter_about(key_list[3], (C, C), C ** -0.5, 0.5),
        "w_bias": draw_w_bias(jax.random.fold_in(key_list[6], 71), part),
        "gain": jnp.clip(1.0 + 0.18 * jax.random.normal(key_list[5], (C,), jnp.float32), 0.1, 1.9),
    }


EPSILON = 1e-05

def normalize(pair, gain):
    values = pair.astype(jnp.float32)
    center = lax.optimization_barrier(jnp.mean(values, axis=-1, keepdims=True))
    spread = lax.optimization_barrier(jnp.mean(jnp.square(values - center), axis=-1, keepdims=True))
    inv_std = lax.rsqrt(spread + EPSILON)
    normed = (values - center) * inv_std
    return ((normed * gain).astype(jnp.bfloat16), normed, inv_std)

def column_grad(tokens, grads, w_qkvg, w_out, bias, scale):
    width = w_out.shape[0]
    heads = bias.shape[0]
    size = width // heads
    count = tokens.shape[0]
    proj = jnp.dot(tokens, w_qkvg, preferred_element_type=jnp.float32)
    queries = proj[:, :width].astype(jnp.bfloat16).reshape(count, heads, size).astype(jnp.float32)
    keys = proj[:, width:2 * width].astype(jnp.bfloat16).reshape(count, heads, size).astype(jnp.float32)
    values = proj[:, 2 * width:3 * width].astype(jnp.bfloat16).reshape(count, heads, size).astype(jnp.float32)
    gate = jax.nn.sigmoid(proj[:, 3 * width:]).reshape(count, heads, size)
    scores = jnp.einsum('khd,ihd->hki', keys, queries) * scale + bias.astype(jnp.float32)
    probs = jax.nn.softmax(scores, axis=1)
    probs_b = probs.astype(jnp.bfloat16).astype(jnp.float32)
    attended = jnp.einsum('hki,khd->ihd', probs_b, values)
    mixed = (gate * attended).astype(jnp.bfloat16).reshape(count, width)
    d_mixed = jnp.dot(grads, w_out.T, preferred_element_type=jnp.float32).reshape(count, heads, size)
    part_wout = jnp.dot(mixed.T, grads, preferred_element_type=jnp.float32)
    d_gate = d_mixed * attended * gate * (1.0 - gate)
    d_att = (d_mixed * gate).astype(jnp.bfloat16).astype(jnp.float32)
    d_values = jnp.einsum('hki,ihd->khd', probs_b, d_att)
    d_probs = jnp.einsum('ihd,khd->hki', d_att, values)
    delta = lax.optimization_barrier(jnp.sum(d_att * attended, axis=-1))
    d_scores = (probs * (d_probs - delta.T[:, None, :])).astype(jnp.bfloat16)
    d_sf = d_scores.astype(jnp.float32)
    d_queries = jnp.einsum('hki,khd->ihd', d_sf, keys) * scale
    d_keys = jnp.einsum('hki,ihd->khd', d_sf, queries) * scale
    d_proj = jnp.concatenate([d_queries.reshape(count, width), d_keys.reshape(count, width), d_values.reshape(count, width), d_gate.reshape(count, width)], axis=1).astype(jnp.bfloat16)
    part_qkvg = jnp.dot(tokens.T, d_proj, preferred_element_type=jnp.float32)
    d_tokens = jnp.dot(d_proj, w_qkvg.T, preferred_element_type=jnp.float32).astype(jnp.bfloat16)
    return (d_tokens, d_scores, part_qkvg, part_wout)

def reference(pair, out_grad, w_qkvg, w_out, w_bias, gain):
    normed_b, normed, inv_std = normalize(pair, gain)
    bias = jnp.einsum('abc,ch->hab', normed_b.astype(jnp.float32), w_bias.astype(jnp.float32)).astype(jnp.bfloat16)
    scale = DH ** (-0.5)
    width = w_out.shape[0]
    heads = w_bias.shape[1]
    length = pair.shape[1]
    inv_count = 1.0 / length

    def step(carry, column):
        d_bias, d_qkvg, d_wout = carry
        tokens = lax.dynamic_index_in_dim(normed_b, column, 1, keepdims=False)
        grads = lax.dynamic_index_in_dim(out_grad, column, 1, keepdims=False)
        d_tokens, d_scores, part_qkvg, part_wout = column_grad(tokens, grads, w_qkvg, w_out, bias, scale)
        return ((d_bias + d_scores.astype(jnp.float32), d_qkvg + part_qkvg, d_wout + part_wout), d_tokens)
    start = (jnp.zeros((heads, length, length), jnp.float32), jnp.zeros((width, 4 * width), jnp.float32), jnp.zeros((width, width), jnp.float32))
    (d_bias, d_qkvg, d_wout), d_cols = lax.scan(step, start, jnp.arange(length, dtype=jnp.int32))
    d_att_x = jnp.swapaxes(d_cols, 0, 1)
    d_bias_x = jnp.einsum('hab,ch->abc', d_bias, w_bias.astype(jnp.float32), precision=lax.Precision.HIGHEST).astype(jnp.bfloat16)
    d_wbias = jnp.einsum('abc,hab->ch', normed_b.astype(jnp.float32), d_bias, precision=lax.Precision.HIGHEST)
    d_xn = d_att_x.astype(jnp.float32) + d_bias_x.astype(jnp.float32)
    d_gain = lax.optimization_barrier(jnp.sum(d_xn * normed, axis=(0, 1)))
    scaled = d_xn * gain
    d_pair = (inv_std * (scaled - lax.optimization_barrier(jnp.mean(scaled, axis=-1, keepdims=True)) - normed * lax.optimization_barrier(jnp.mean(scaled * normed, axis=-1, keepdims=True)))).astype(jnp.bfloat16)
    return (d_pair, d_qkvg * inv_count, d_wout * inv_count, d_wbias * inv_count, d_gain * inv_count)
```

```python
import functools

import jax
import jax.numpy as jnp
from jax import lax
from jax.experimental import pallas as pl
from jax.experimental.pallas import tpu as pltpu
from jax.sharding import PartitionSpec as P

DH = 32


EPSILON = 1e-05


def normalize(pair, gain):
    values = pair.astype(jnp.float32)
    center = jnp.mean(values, axis=-1, keepdims=True)
    spread = jnp.mean(jnp.square(values - center), axis=-1, keepdims=True)
    inv_std = lax.rsqrt(spread + EPSILON)
    normed = (values - center) * inv_std
    return ((normed * gain).astype(jnp.bfloat16), normed, inv_std)


def column_grad(tokens, grads, w_qkvg, w_out, bias, scale):
    width = w_out.shape[0]
    heads = bias.shape[0]
    size = width // heads
    count = tokens.shape[0]
    proj = jnp.dot(tokens, w_qkvg, preferred_element_type=jnp.float32)
    queries = proj[:, :width].astype(jnp.bfloat16).reshape(count, heads, size)
    keys = proj[:, width : 2 * width].astype(jnp.bfloat16).reshape(count, heads, size)
    values = proj[:, 2 * width : 3 * width].astype(jnp.bfloat16).reshape(count, heads, size)
    gate = jax.nn.sigmoid(proj[:, 3 * width :]).reshape(count, heads, size)
    scores = jnp.einsum("khd,ihd->hki", keys, queries, preferred_element_type=jnp.float32) * scale
    scores = scores + bias.astype(jnp.float32)
    probs = jax.nn.softmax(scores, axis=1)
    probs_b = probs.astype(jnp.bfloat16)
    attended = jnp.einsum("hki,khd->ihd", probs_b, values, preferred_element_type=jnp.float32)
    mixed = (gate * attended).astype(jnp.bfloat16).reshape(count, width)
    d_mixed = lax.dot_general(
        grads, w_out, (((1,), (1,)), ((), ())), preferred_element_type=jnp.float32
    ).reshape(count, heads, size)
    part_wout = lax.dot_general(
        mixed, grads, (((0,), (0,)), ((), ())), preferred_element_type=jnp.float32
    )
    d_gate = d_mixed * attended * gate * (1.0 - gate)
    d_att = (d_mixed * gate).astype(jnp.bfloat16)
    d_values = jnp.einsum("hki,ihd->khd", probs_b, d_att, preferred_element_type=jnp.float32)
    d_probs = jnp.einsum("ihd,khd->hki", d_att, values, preferred_element_type=jnp.float32)
    delta = jnp.sum(d_att.astype(jnp.float32) * attended, axis=-1)
    d_scores = (probs * (d_probs - delta.T[:, None, :])).astype(jnp.bfloat16)
    d_queries = (
        jnp.einsum("hki,khd->ihd", d_scores, keys, preferred_element_type=jnp.float32) * scale
    )
    d_keys = (
        jnp.einsum("hki,ihd->khd", d_scores, queries, preferred_element_type=jnp.float32) * scale
    )
    d_proj = jnp.concatenate(
        [
            d_queries.reshape(count, width),
            d_keys.reshape(count, width),
            d_values.reshape(count, width),
            d_gate.reshape(count, width),
        ],
        axis=1,
    ).astype(jnp.bfloat16)
    part_qkvg = lax.dot_general(
        tokens, d_proj, (((0,), (0,)), ((), ())), preferred_element_type=jnp.float32
    )
    d_tokens = lax.dot_general(
        d_proj, w_qkvg, (((1,), (1,)), ((), ())), preferred_element_type=jnp.float32
    ).astype(jnp.bfloat16)
    return (d_tokens, d_scores, part_qkvg, part_wout, queries, keys, values, d_att, delta)


def sharded_plan(pair, out_grad, w_qkvg, w_out, w_bias, gain):
    normed_b, normed, inv_std = normalize(pair, gain)
    width = w_out.shape[0]
    heads = w_bias.shape[1]
    scale = DH ** (-0.5)
    columns = lax.all_to_all(normed_b, "row", split_axis=1, concat_axis=0, tiled=True)
    wide_bias = w_bias.astype(jnp.float32)
    local_bias = jnp.einsum(
        "abc,ch->hab", normed_b, w_bias, preferred_element_type=jnp.float32
    ).astype(jnp.bfloat16)
    bias = lax.all_gather(local_bias, "row", axis=1, tiled=True)
    length = bias.shape[1]
    inv_count = 1.0 / length
    inputs = (jnp.swapaxes(columns, 0, 1), jnp.swapaxes(out_grad, 0, 1))

    def step(carry, pieces):
        d_bias, d_qkvg, d_wout = carry
        outs = column_grad(pieces[0], pieces[1], w_qkvg, w_out, bias, scale)
        return ((d_bias + outs[1].astype(jnp.float32), d_qkvg + outs[2], d_wout + outs[3]), outs[0])

    start = (
        jnp.zeros((heads, length, length), jnp.float32),
        jnp.zeros((width, 4 * width), jnp.float32),
        jnp.zeros((width, width), jnp.float32),
    )
    (d_bias, d_qkvg, d_wout), d_cols = lax.scan(step, start, inputs)
    d_att_cols = jnp.swapaxes(d_cols, 0, 1)
    owned = lax.psum_scatter(d_bias, "row", scatter_dimension=1, tiled=True)
    d_att_x = lax.all_to_all(d_att_cols, "row", split_axis=0, concat_axis=1, tiled=True)
    d_bias_x = jnp.einsum("hab,ch->abc", owned, wide_bias, precision=lax.Precision.HIGHEST).astype(
        jnp.bfloat16
    )
    d_wbias = jnp.einsum(
        "abc,hab->ch", normed_b.astype(jnp.float32), owned, precision=lax.Precision.HIGHEST
    )
    d_xn = d_att_x.astype(jnp.float32) + d_bias_x.astype(jnp.float32)
    local_gain = jnp.sum(d_xn * normed, axis=(0, 1))
    scaled = d_xn * gain
    d_pair = (
        inv_std
        * (
            scaled
            - jnp.mean(scaled, axis=-1, keepdims=True)
            - normed * jnp.mean(scaled * normed, axis=-1, keepdims=True)
        )
    ).astype(jnp.bfloat16)
    total_qkvg, total_wout, total_wbias, total_gain = lax.psum(
        (d_qkvg, d_wout, d_wbias, local_gain), "row"
    )
    return (
        d_pair,
        total_qkvg * inv_count,
        total_wout * inv_count,
        total_wbias * inv_count,
        total_gain * inv_count,
    )


BLOCK = 128
MASKED = -1e30
BF16 = jnp.bfloat16
F32 = jnp.float32


def mm(a, b, dims=(1, 0)):
    return lax.dot_general(
        a, b, (((dims[0],), (dims[1],)), ((), ())), preferred_element_type=F32
    )


def log2(value):
    return value.bit_length() - 1


def exchange(n, pair_ref, grad_ref, pairs_ref, grads_ref, send_sems, recv_sems, local_sems):
    me = lax.axis_index("row")
    barrier = pltpu.get_barrier_semaphore()
    for offset in range(1, n):
        pl.semaphore_signal(
            barrier,
            inc=1,
            device_id={"row": lax.rem(me + offset, n)},
            device_id_type=pl.DeviceIdType.MESH,
        )
    own = [
        pltpu.make_async_copy(pair_ref, pairs_ref.at[me], local_sems.at[0]),
        pltpu.make_async_copy(grad_ref, grads_ref.at[me], local_sems.at[1]),
    ]
    for copy in own:
        copy.start()
    pl.semaphore_wait(barrier, n - 1)
    copies = []
    for kind, (src, dst) in enumerate(((pair_ref, pairs_ref), (grad_ref, grads_ref))):
        for offset in range(1, n):
            copy = pltpu.make_async_remote_copy(
                src_ref=src,
                dst_ref=dst.at[me],
                send_sem=send_sems.at[kind, offset],
                recv_sem=recv_sems.at[kind, offset],
                device_id={"row": lax.rem(me + offset, n)},
                device_id_type=pl.DeviceIdType.MESH,
            )
            copy.start()
            copies.append(copy)
    for copy in own + copies:
        copy.wait()


def whole_crop(
    local,
    pairs_ref,
    grads_ref,
    w_qkvg_ref,
    w_out_ref,
    w_bias_ref,
    gain_ref,
    d_pair_ref,
    d_qkvg_ref,
    d_wout_ref,
    d_wbias_ref,
    d_gain_ref,
    d_xn_ref,
    normed_ref,
    inv_ref,
):
    me = lax.axis_index("row")
    chunk = pairs_ref.shape[1]
    width = pairs_ref.shape[2]
    heads = w_bias_ref.shape[0]
    size = width // heads
    length = chunk // local
    cells = length * length
    scale = size ** (-0.5)
    inv_count = 1.0 / length
    s_local, s_length, s_chunk = log2(local), log2(length), log2(chunk)

    def iota(shape, axis):
        return lax.broadcasted_iota(jnp.int32, shape, axis)

    def row_of(position):
        return (position & (chunk - 1)) >> s_local

    g, r = iota((cells, cells), 0), iota((cells, cells), 1)
    cell = (row_of(g) << s_length) + ((g >> s_chunk) << s_local) + (g & (local - 1))
    permute = (cell == r).astype(F32).astype(BF16)
    p, q = iota((BLOCK, BLOCK), 0), iota((BLOCK, BLOCK), 1)
    same_column = ((p >> s_chunk) == (q >> s_chunk)) & (((p ^ q) & (local - 1)) == 0)
    p, r = iota((BLOCK, cells), 0), iota((BLOCK, cells), 1)
    spread_key = (row_of(p) == (r >> s_length)).astype(F32).astype(BF16)
    r, p = iota((cells, BLOCK), 0), iota((cells, BLOCK), 1)
    pick_key = (row_of(p) == (r >> s_length)).astype(F32).astype(BF16)
    pick_query = row_of(p) == (r & (length - 1))
    lane_head = iota((BLOCK, width), 1) >> log2(size)

    def per_head(block):
        zero = jnp.zeros_like(block)
        return jnp.concatenate([jnp.where(lane_head == h, block, zero) for h in range(heads)], 0)

    def own_head(stacked):
        out = stacked[:BLOCK]
        for h in range(1, heads):
            out = jnp.where(lane_head == h, stacked[h * BLOCK : (h + 1) * BLOCK], out)
        return out

    w_bias = w_bias_ref[...]
    w_bias_rows = jnp.concatenate(
        [jnp.broadcast_to(w_bias[h : h + 1], (BLOCK, width)) for h in range(heads)], 0
    ).astype(BF16)
    w_qkvg = w_qkvg_ref[...]
    w_out = w_out_ref[...]
    gain = gain_ref[...]

    values = pairs_ref[...].reshape(cells, width).astype(F32)
    center = jnp.mean(values, axis=-1, keepdims=True)
    spread = jnp.mean(jnp.square(values - center), axis=-1, keepdims=True)
    inv_std = lax.rsqrt(spread + EPSILON)
    normed = (values - center) * inv_std
    xn = (normed * gain).astype(BF16)
    normed_ref[...] = normed
    inv_ref[...] = jnp.broadcast_to(inv_std, (cells, width))

    tokens = mm(permute, xn).astype(BF16)
    proj = mm(tokens, w_qkvg)
    bias_cells = mm(xn, w_bias_rows, (1, 1))
    bias = mm(
        spread_key,
        jnp.concatenate(
            [
                jnp.where(pick_query, bias_cells[:, h * BLOCK : (h + 1) * BLOCK], 0.0)
                for h in range(heads)
            ],
            1,
        ).astype(BF16),
    )
    bias = jnp.concatenate(
        [
            jnp.where(same_column, bias[:, h * BLOCK : (h + 1) * BLOCK], MASKED)
            for h in range(heads)
        ],
        0,
    )
    grads = grads_ref[...].reshape(cells, width)
    d_mixed_all = mm(grads, w_out, (1, 1))

    mixed_parts, d_proj_parts = [], []
    d_bias_x = jnp.zeros((cells, width), F32)
    d_wbias = jnp.zeros((heads * BLOCK, width), F32)
    for start in range(0, cells, BLOCK):
        rows = slice(start, start + BLOCK)
        queries = proj[rows, :width].astype(BF16)
        keys = per_head(proj[rows, width : 2 * width]).astype(BF16)
        vals = per_head(proj[rows, 2 * width : 3 * width]).astype(BF16)
        gate = jax.nn.sigmoid(proj[rows, 3 * width :])
        scores = mm(keys, queries, (1, 1)) * scale + bias
        scores = scores.reshape(heads, BLOCK, BLOCK)
        top = jnp.max(scores, axis=1, keepdims=True)
        weights = jnp.exp(scores - top)
        probs = weights / jnp.sum(weights, axis=1, keepdims=True)
        probs_b = probs.astype(BF16)
        flat_b = probs_b.reshape(heads * BLOCK, BLOCK)
        attended = mm(flat_b, vals, (0, 0))
        d_mixed = d_mixed_all[rows]
        mixed_parts.append((gate * attended).astype(BF16))
        d_gate = d_mixed * attended * gate * (1.0 - gate)
        d_att = (d_mixed * gate).astype(BF16)
        d_values = own_head(mm(flat_b, d_att))
        d_probs = mm(vals, d_att, (1, 1)).reshape(heads, BLOCK, BLOCK)
        delta = jnp.sum(probs_b.astype(F32) * d_probs, axis=1, keepdims=True)
        d_scores = (probs * (d_probs - delta)).astype(BF16)
        flat_d = d_scores.reshape(heads * BLOCK, BLOCK)
        d_queries = mm(flat_d, keys, (0, 0)) * scale
        d_keys = own_head(mm(flat_d, queries)) * scale
        d_proj_parts.append(
            jnp.concatenate([d_queries, d_keys, d_values, d_gate], 1).astype(BF16)
        )
        terms = mm(pick_key, jnp.concatenate([d_scores[h] for h in range(heads)], 1))
        terms = jnp.concatenate(
            [
                jnp.where(pick_query, terms[:, h * BLOCK : (h + 1) * BLOCK], 0.0)
                for h in range(heads)
            ],
            1,
        ).astype(BF16)
        d_bias_x = d_bias_x + mm(terms, w_bias_rows)
        d_wbias = d_wbias + mm(terms, xn, (0, 0))

    d_proj = jnp.concatenate(d_proj_parts, 0)
    mixed = jnp.concatenate(mixed_parts, 0)
    d_qkvg_ref[...] = mm(tokens, d_proj, (0, 0)) * inv_count
    d_wout_ref[...] = mm(mixed, grads, (0, 0)) * inv_count
    d_wbias_ref[...] = jnp.sum(d_wbias.reshape(heads, BLOCK, width), axis=1) * inv_count
    d_tokens = mm(d_proj, w_qkvg, (1, 1)).astype(BF16)
    d_xn = mm(permute, d_tokens, (0, 0)) + d_bias_x.astype(BF16).astype(F32)
    d_gain_ref[...] = jnp.sum(d_xn * normed, axis=0, keepdims=True) * inv_count
    d_xn_ref[...] = d_xn

    own = pl.ds(pl.multiple_of(me * chunk, chunk), chunk)
    normed = normed_ref[own, :]
    scaled = d_xn_ref[own, :] * gain
    d_pair = inv_ref[own, :] * (
        scaled
        - jnp.mean(scaled, axis=-1, keepdims=True)
        - normed * jnp.mean(scaled * normed, axis=-1, keepdims=True)
    )
    d_pair_ref[...] = d_pair.astype(BF16).reshape(d_pair_ref.shape)


def gathered_plan(n, pair, out_grad, w_qkvg, w_out, w_bias, gain):
    local, length, width = pair.shape
    heads = w_bias.shape[1]
    cells = length * length
    chunk = local * length
    vmem = pl.BlockSpec(memory_space=pltpu.VMEM)
    hbm = pl.BlockSpec(memory_space=pl.ANY)
    pairs, grads = pl.pallas_call(
        functools.partial(exchange, n),
        out_shape=[jax.ShapeDtypeStruct((n, chunk, width), BF16)] * 2,
        in_specs=[hbm] * 2,
        out_specs=[vmem] * 2,
        scratch_shapes=[
            pltpu.SemaphoreType.DMA((2, n)),
            pltpu.SemaphoreType.DMA((2, n)),
            pltpu.SemaphoreType.DMA((2,)),
        ],
        compiler_params=pltpu.CompilerParams(collective_id=0, has_side_effects=True),
    )(pair.reshape(chunk, width), out_grad.reshape(chunk, width))
    d_pair, d_qkvg, d_wout, d_wbias, d_gain = pl.pallas_call(
        functools.partial(whole_crop, local),
        out_shape=[
            jax.ShapeDtypeStruct(pair.shape, BF16),
            jax.ShapeDtypeStruct(w_qkvg.shape, F32),
            jax.ShapeDtypeStruct(w_out.shape, F32),
            jax.ShapeDtypeStruct((heads, width), F32),
            jax.ShapeDtypeStruct((1, width), F32),
        ],
        in_specs=[vmem] * 6,
        out_specs=[vmem] * 5,
        scratch_shapes=[pltpu.VMEM((cells, width), F32)] * 3,
        compiler_params=pltpu.CompilerParams(vmem_limit_bytes=32 * 1024 * 1024),
    )(pairs, grads, w_qkvg, w_out, w_bias.T, gain.reshape(1, width))
    return (d_pair, d_qkvg, d_wout, d_wbias.T, d_gain.reshape(width))


def per_device(n, pair, out_grad, w_qkvg, w_out, w_bias, gain):
    local, length, width = pair.shape
    chunk = local * length
    powers = all(size & (size - 1) == 0 for size in (local, length, width, w_bias.shape[1]))
    fits = n > 1 and width == BLOCK and chunk % 16 == 0 and BLOCK % chunk == 0
    if powers and fits and length * length % BLOCK == 0 and length <= 32:
        return gathered_plan(n, pair, out_grad, w_qkvg, w_out, w_bias, gain)
    return sharded_plan(pair, out_grad, w_qkvg, w_out, w_bias, gain)


def solution(mesh):
    in_specs = (P(("crop", "row"), None, None), P("crop", "row", None), P(), P(), P(), P())
    out_specs = (
        P(("crop", "row"), None, None),
        P("crop", None),
        P("crop", None),
        P("crop", None),
        P("crop"),
    )
    return jax.shard_map(
        functools.partial(per_device, mesh.shape["row"]),
        mesh=mesh,
        in_specs=in_specs, out_specs=out_specs, check_vma=False
    )
```

```python
import functools

import jax
import jax.numpy as jnp
from jax import lax
from jax.experimental import pallas as pl
from jax.experimental.pallas import tpu as pltpu
from jax.sharding import PartitionSpec as P

DH = 32


EPSILON = 1e-05


def normalize(pair, gain):
    values = pair.astype(jnp.float32)
    center = jnp.mean(values, axis=-1, keepdims=True)
    spread = jnp.mean(jnp.square(values - center), axis=-1, keepdims=True)
    inv_std = lax.rsqrt(spread + EPSILON)
    normed = (values - center) * inv_std
    return ((normed * gain).astype(jnp.bfloat16), normed, inv_std)


def column_grad(tokens, grads, w_qkvg, w_out, bias, scale):
    width = w_out.shape[0]
    heads = bias.shape[0]
    size = width // heads
    count = tokens.shape[0]
    proj = jnp.dot(tokens, w_qkvg, preferred_element_type=jnp.float32)
    queries = proj[:, :width].astype(jnp.bfloat16).reshape(count, heads, size)
    keys = proj[:, width : 2 * width].astype(jnp.bfloat16).reshape(count, heads, size)
    values = proj[:, 2 * width : 3 * width].astype(jnp.bfloat16).reshape(count, heads, size)
    gate = jax.nn.sigmoid(proj[:, 3 * width :]).reshape(count, heads, size)
    scores = jnp.einsum("khd,ihd->hki", keys, queries, preferred_element_type=jnp.float32) * scale
    scores = scores + bias.astype(jnp.float32)
    probs = jax.nn.softmax(scores, axis=1)
    probs_b = probs.astype(jnp.bfloat16)
    attended = jnp.einsum("hki,khd->ihd", probs_b, values, preferred_element_type=jnp.float32)
    mixed = (gate * attended).astype(jnp.bfloat16).reshape(count, width)
    d_mixed = lax.dot_general(
        grads, w_out, (((1,), (1,)), ((), ())), preferred_element_type=jnp.float32
    ).reshape(count, heads, size)
    part_wout = lax.dot_general(
        mixed, grads, (((0,), (0,)), ((), ())), preferred_element_type=jnp.float32
    )
    d_gate = d_mixed * attended * gate * (1.0 - gate)
    d_att = (d_mixed * gate).astype(jnp.bfloat16)
    d_values = jnp.einsum("hki,ihd->khd", probs_b, d_att, preferred_element_type=jnp.float32)
    d_probs = jnp.einsum("ihd,khd->hki", d_att, values, preferred_element_type=jnp.float32)
    delta = jnp.sum(d_att.astype(jnp.float32) * attended, axis=-1)
    d_scores = (probs * (d_probs - delta.T[:, None, :])).astype(jnp.bfloat16)
    d_queries = (
        jnp.einsum("hki,khd->ihd", d_scores, keys, preferred_element_type=jnp.float32) * scale
    )
    d_keys = (
        jnp.einsum("hki,ihd->khd", d_scores, queries, preferred_element_type=jnp.float32) * scale
    )
    d_proj = jnp.concatenate(
        [
            d_queries.reshape(count, width),
            d_keys.reshape(count, width),
            d_values.reshape(count, width),
            d_gate.reshape(count, width),
        ],
        axis=1,
    ).astype(jnp.bfloat16)
    part_qkvg = lax.dot_general(
        tokens, d_proj, (((0,), (0,)), ((), ())), preferred_element_type=jnp.float32
    )
    d_tokens = lax.dot_general(
        d_proj, w_qkvg, (((1,), (1,)), ((), ())), preferred_element_type=jnp.float32
    ).astype(jnp.bfloat16)
    return (d_tokens, d_scores, part_qkvg, part_wout, queries, keys, values, d_att, delta)


def sharded_plan(pair, out_grad, w_qkvg, w_out, w_bias, gain):
    normed_b, normed, inv_std = normalize(pair, gain)
    width = w_out.shape[0]
    heads = w_bias.shape[1]
    scale = DH ** (-0.5)
    columns = lax.all_to_all(normed_b, "row", split_axis=1, concat_axis=0, tiled=True)
    wide_bias = w_bias.astype(jnp.float32)
    local_bias = jnp.einsum(
        "abc,ch->hab", normed_b, w_bias, preferred_element_type=jnp.float32
    ).astype(jnp.bfloat16)
    bias = lax.all_gather(local_bias, "row", axis=1, tiled=True)
    length = bias.shape[1]
    inv_count = 1.0 / length
    inputs = (jnp.swapaxes(columns, 0, 1), jnp.swapaxes(out_grad, 0, 1))

    def step(carry, pieces):
        d_bias, d_qkvg, d_wout = carry
        outs = column_grad(pieces[0], pieces[1], w_qkvg, w_out, bias, scale)
        return ((d_bias + outs[1].astype(jnp.float32), d_qkvg + outs[2], d_wout + outs[3]), outs[0])

    start = (
        jnp.zeros((heads, length, length), jnp.float32),
        jnp.zeros((width, 4 * width), jnp.float32),
        jnp.zeros((width, width), jnp.float32),
    )
    (d_bias, d_qkvg, d_wout), d_cols = lax.scan(step, start, inputs)
    d_att_cols = jnp.swapaxes(d_cols, 0, 1)
    owned = lax.psum_scatter(d_bias, "row", scatter_dimension=1, tiled=True)
    d_att_x = lax.all_to_all(d_att_cols, "row", split_axis=0, concat_axis=1, tiled=True)
    d_bias_x = jnp.einsum("hab,ch->abc", owned, wide_bias, precision=lax.Precision.HIGHEST).astype(
        jnp.bfloat16
    )
    d_wbias = jnp.einsum(
        "abc,hab->ch", normed_b.astype(jnp.float32), owned, precision=lax.Precision.HIGHEST
    )
    d_xn = d_att_x.astype(jnp.float32) + d_bias_x.astype(jnp.float32)
    local_gain = jnp.sum(d_xn * normed, axis=(0, 1))
    scaled = d_xn * gain
    d_pair = (
        inv_std
        * (
            scaled
            - jnp.mean(scaled, axis=-1, keepdims=True)
            - normed * jnp.mean(scaled * normed, axis=-1, keepdims=True)
        )
    ).astype(jnp.bfloat16)
    total_qkvg, total_wout, total_wbias, total_gain = lax.psum(
        (d_qkvg, d_wout, d_wbias, local_gain), "row"
    )
    return (
        d_pair,
        total_qkvg * inv_count,
        total_wout * inv_count,
        total_wbias * inv_count,
        total_gain * inv_count,
    )


BLOCK = 128
VMEM_LIMIT = 60 * 1024 * 1024
MASKED = -1e30
BF16 = jnp.bfloat16
F32 = jnp.float32


def mm(a, b, dims=(1, 0)):
    return lax.dot_general(
        a, b, (((dims[0],), (dims[1],)), ((), ())), preferred_element_type=F32
    )


def log2(value):
    return value.bit_length() - 1


def whole_crop(
    n,
    local,
    pair_hbm,
    grad_hbm,
    w_qkvg_hbm,
    w_out_hbm,
    w_bias_hbm,
    gain_hbm,
    d_pair_ref,
    d_qkvg_ref,
    d_wout_ref,
    d_wbias_ref,
    d_gain_ref,
    pairs_ref,
    grads_ref,
    w_qkvg_ref,
    w_out_ref,
    w_bias_ref,
    gain_ref,
    d_xn_ref,
    normed_ref,
    inv_ref,
    send_sems,
    recv_sems,
    local_sems,
):
    me = lax.axis_index("row")
    barrier = pltpu.get_barrier_semaphore()
    for offset in range(1, n):
        pl.semaphore_signal(
            barrier,
            inc=1,
            device_id={"row": lax.rem(me + offset, n)},
            device_id_type=pl.DeviceIdType.MESH,
        )
    staged = [
        pltpu.make_async_copy(src, dst, local_sems.at[index])
        for index, (src, dst) in enumerate(
            (
                (pair_hbm, pairs_ref.at[me]),
                (gain_hbm, gain_ref),
                (w_qkvg_hbm, w_qkvg_ref),
                (w_bias_hbm, w_bias_ref),
                (grad_hbm, grads_ref.at[me]),
                (w_out_hbm, w_out_ref),
            )
        )
    ]
    for copy in staged:
        copy.start()
    pl.semaphore_wait(barrier, n - 1)
    sent = []
    for kind, (src, dst) in enumerate(((pair_hbm, pairs_ref), (grad_hbm, grads_ref))):
        for offset in range(1, n):
            copy = pltpu.make_async_remote_copy(
                src_ref=src,
                dst_ref=dst.at[me],
                send_sem=send_sems.at[kind, offset],
                recv_sem=recv_sems.at[kind, offset],
                device_id={"row": lax.rem(me + offset, n)},
                device_id_type=pl.DeviceIdType.MESH,
            )
            copy.start()
            sent.append(copy)

    chunk = pairs_ref.shape[1]
    width = pairs_ref.shape[2]
    heads = w_bias_ref.shape[0]
    size = width // heads
    length = chunk // local
    cells = length * length
    scale = size ** (-0.5)
    inv_count = 1.0 / length
    s_local, s_length, s_chunk = log2(local), log2(length), log2(chunk)

    def iota(shape, axis):
        return lax.broadcasted_iota(jnp.int32, shape, axis)

    def row_of(position):
        return (position & (chunk - 1)) >> s_local

    g, r = iota((cells, cells), 0), iota((cells, cells), 1)
    cell = (row_of(g) << s_length) + ((g >> s_chunk) << s_local) + (g & (local - 1))
    permute = (cell == r).astype(F32).astype(BF16)
    p, q = iota((BLOCK, BLOCK), 0), iota((BLOCK, BLOCK), 1)
    same_column = ((p >> s_chunk) == (q >> s_chunk)) & (((p ^ q) & (local - 1)) == 0)
    p, r = iota((BLOCK, cells), 0), iota((BLOCK, cells), 1)
    spread_key = (row_of(p) == (r >> s_length)).astype(F32).astype(BF16)
    r, p = iota((cells, BLOCK), 0), iota((cells, BLOCK), 1)
    pick_key = (row_of(p) == (r >> s_length)).astype(F32).astype(BF16)
    pick_query = row_of(p) == (r & (length - 1))
    lane_head = iota((BLOCK, width), 1) >> log2(size)

    def per_head(block):
        zero = jnp.zeros_like(block)
        return jnp.concatenate([jnp.where(lane_head == h, block, zero) for h in range(heads)], 0)

    def own_head(stacked):
        out = stacked[:BLOCK]
        for h in range(1, heads):
            out = jnp.where(lane_head == h, stacked[h * BLOCK : (h + 1) * BLOCK], out)
        return out

    for copy in staged[:4]:
        copy.wait()
    for copy in sent[: n - 1]:
        copy.wait_recv()

    w_bias = w_bias_ref[...]
    w_bias_rows = jnp.concatenate(
        [jnp.broadcast_to(w_bias[h : h + 1], (BLOCK, width)) for h in range(heads)], 0
    ).astype(BF16)
    w_qkvg = w_qkvg_ref[...]
    gain = gain_ref[...]

    values = pairs_ref[...].reshape(cells, width).astype(F32)
    center = jnp.mean(values, axis=-1, keepdims=True)
    spread = jnp.mean(jnp.square(values - center), axis=-1, keepdims=True)
    inv_std = lax.rsqrt(spread + EPSILON)
    normed = (values - center) * inv_std
    xn = (normed * gain).astype(BF16)
    normed_ref[...] = normed
    inv_ref[...] = jnp.broadcast_to(inv_std, (cells, width))

    tokens = mm(permute, xn).astype(BF16)
    proj = mm(tokens, w_qkvg)
    bias_cells = mm(xn, w_bias_rows, (1, 1))
    bias = mm(
        spread_key,
        jnp.concatenate(
            [
                jnp.where(pick_query, bias_cells[:, h * BLOCK : (h + 1) * BLOCK], 0.0)
                for h in range(heads)
            ],
            1,
        ).astype(BF16),
    )
    bias = jnp.concatenate(
        [
            jnp.where(same_column, bias[:, h * BLOCK : (h + 1) * BLOCK], MASKED)
            for h in range(heads)
        ],
        0,
    )
    forward = []
    for start in range(0, cells, BLOCK):
        rows = slice(start, start + BLOCK)
        queries = proj[rows, :width].astype(BF16)
        keys = per_head(proj[rows, width : 2 * width]).astype(BF16)
        vals = per_head(proj[rows, 2 * width : 3 * width]).astype(BF16)
        gate = jax.nn.sigmoid(proj[rows, 3 * width :])
        scores = mm(keys, queries, (1, 1)) * scale + bias
        scores = scores.reshape(heads, BLOCK, BLOCK)
        top = jnp.max(scores, axis=1, keepdims=True)
        weights = jnp.exp(scores - top)
        probs = weights / jnp.sum(weights, axis=1, keepdims=True)
        probs_b = probs.astype(BF16)
        flat_b = probs_b.reshape(heads * BLOCK, BLOCK)
        attended = mm(flat_b, vals, (0, 0))
        forward.append((queries, keys, vals, gate, probs, probs_b, attended))

    for copy in staged[4:]:
        copy.wait()
    for copy in sent[n - 1 :]:
        copy.wait_recv()
    grads = grads_ref[...].reshape(cells, width)
    d_mixed_all = mm(grads, w_out_ref[...], (1, 1))

    mixed_parts, d_proj_parts = [], []
    d_bias_x = jnp.zeros((cells, width), F32)
    d_wbias = jnp.zeros((heads * BLOCK, width), F32)
    for start in range(0, cells, BLOCK):
        queries, keys, vals, gate, probs, probs_b, attended = forward[start // BLOCK]
        rows = slice(start, start + BLOCK)
        flat_b = probs_b.reshape(heads * BLOCK, BLOCK)
        d_mixed = d_mixed_all[rows]
        mixed_parts.append((gate * attended).astype(BF16))
        d_gate = d_mixed * attended * gate * (1.0 - gate)
        d_att = (d_mixed * gate).astype(BF16)
        d_values = own_head(mm(flat_b, d_att))
        d_probs = mm(vals, d_att, (1, 1)).reshape(heads, BLOCK, BLOCK)
        delta = jnp.sum(probs_b.astype(F32) * d_probs, axis=1, keepdims=True)
        d_scores = (probs * (d_probs - delta)).astype(BF16)
        flat_d = d_scores.reshape(heads * BLOCK, BLOCK)
        d_queries = mm(flat_d, keys, (0, 0)) * scale
        d_keys = own_head(mm(flat_d, queries)) * scale
        d_proj_parts.append(
            jnp.concatenate([d_queries, d_keys, d_values, d_gate], 1).astype(BF16)
        )
        terms = mm(pick_key, jnp.concatenate([d_scores[h] for h in range(heads)], 1))
        terms = jnp.concatenate(
            [
                jnp.where(pick_query, terms[:, h * BLOCK : (h + 1) * BLOCK], 0.0)
                for h in range(heads)
            ],
            1,
        ).astype(BF16)
        d_bias_x = d_bias_x + mm(terms, w_bias_rows)
        d_wbias = d_wbias + mm(terms, xn, (0, 0))

    d_proj = jnp.concatenate(d_proj_parts, 0)
    mixed = jnp.concatenate(mixed_parts, 0)
    d_qkvg_ref[...] = mm(tokens, d_proj, (0, 0)) * inv_count
    d_wout_ref[...] = mm(mixed, grads, (0, 0)) * inv_count
    d_wbias_ref[...] = jnp.sum(d_wbias.reshape(heads, BLOCK, width), axis=1) * inv_count
    d_tokens = mm(d_proj, w_qkvg, (1, 1)).astype(BF16)
    d_xn = mm(permute, d_tokens, (0, 0)) + d_bias_x.astype(BF16).astype(F32)
    d_gain_ref[...] = jnp.sum(d_xn * normed, axis=0, keepdims=True) * inv_count
    d_xn_ref[...] = d_xn

    own = pl.ds(pl.multiple_of(me * chunk, chunk), chunk)
    normed = normed_ref[own, :]
    scaled = d_xn_ref[own, :] * gain
    d_pair = inv_ref[own, :] * (
        scaled
        - jnp.mean(scaled, axis=-1, keepdims=True)
        - normed * jnp.mean(scaled * normed, axis=-1, keepdims=True)
    )
    d_pair_ref[...] = d_pair.astype(BF16).reshape(d_pair_ref.shape)
    for copy in sent:
        copy.wait_send()


def deliver(count, *refs):
    copies = [
        pltpu.make_async_copy(refs[index], refs[count + index], refs[-1].at[index])
        for index in range(count)
    ]
    for copy in copies:
        copy.start()
    for copy in copies:
        copy.wait()


def gathered_plan(n, pair, out_grad, w_qkvg, w_out, w_bias, gain):
    local, length, width = pair.shape
    heads = w_bias.shape[1]
    cells = length * length
    chunk = local * length
    vmem = pl.BlockSpec(memory_space=pltpu.VMEM)
    hbm = pl.BlockSpec(memory_space=pltpu.HBM)
    anywhere = pl.BlockSpec(memory_space=pl.ANY)
    shapes = [
        jax.ShapeDtypeStruct(pair.shape, BF16),
        jax.ShapeDtypeStruct(w_qkvg.shape, F32),
        jax.ShapeDtypeStruct(w_out.shape, F32),
        jax.ShapeDtypeStruct((heads, width), F32),
        jax.ShapeDtypeStruct((1, width), F32),
    ]
    results = pl.pallas_call(
        functools.partial(whole_crop, n, local),
        out_shape=shapes,
        in_specs=[hbm] * 6,
        out_specs=[vmem] * 5,
        scratch_shapes=[
            pltpu.VMEM((n, chunk, width), BF16),
            pltpu.VMEM((n, chunk, width), BF16),
            pltpu.VMEM(w_qkvg.shape, BF16),
            pltpu.VMEM(w_out.shape, BF16),
            pltpu.VMEM((heads, width), BF16),
            pltpu.VMEM((1, width), F32),
            pltpu.VMEM((cells, width), F32),
            pltpu.VMEM((cells, width), F32),
            pltpu.VMEM((cells, width), F32),
            pltpu.SemaphoreType.DMA((2, n)),
            pltpu.SemaphoreType.DMA((2, n)),
            pltpu.SemaphoreType.DMA((6,)),
        ],
        compiler_params=pltpu.CompilerParams(
            collective_id=0, has_side_effects=True, vmem_limit_bytes=VMEM_LIMIT
        ),
    )(
        pair.reshape(chunk, width),
        out_grad.reshape(chunk, width),
        w_qkvg,
        w_out,
        w_bias.T,
        gain.reshape(1, width),
    )
    results = pl.pallas_call(
        functools.partial(deliver, len(shapes)),
        out_shape=shapes,
        in_specs=[anywhere] * len(shapes),
        out_specs=[hbm] * len(shapes),
        scratch_shapes=[pltpu.SemaphoreType.DMA((len(shapes),))],
        compiler_params=pltpu.CompilerParams(vmem_limit_bytes=VMEM_LIMIT),
    )(*results)
    d_pair, d_qkvg, d_wout, d_wbias, d_gain = results
    return (d_pair, d_qkvg, d_wout, d_wbias.T, d_gain.reshape(width))


def per_device(n, pair, out_grad, w_qkvg, w_out, w_bias, gain):
    local, length, width = pair.shape
    chunk = local * length
    powers = all(size & (size - 1) == 0 for size in (local, length, width, w_bias.shape[1]))
    fits = n > 1 and width == BLOCK and chunk % 16 == 0 and BLOCK % chunk == 0
    if powers and fits and length * length % BLOCK == 0 and length <= 32:
        return gathered_plan(n, pair, out_grad, w_qkvg, w_out, w_bias, gain)
    return sharded_plan(pair, out_grad, w_qkvg, w_out, w_bias, gain)


def solution(mesh):
    in_specs = (P(("crop", "row"), None, None), P("crop", "row", None), P(), P(), P(), P())
    out_specs = (
        P(("crop", "row"), None, None),
        P("crop", None),
        P("crop", None),
        P("crop", None),
        P("crop"),
    )
    return jax.shard_map(
        functools.partial(per_device, mesh.shape["row"]),
        mesh=mesh,
        in_specs=in_specs, out_specs=out_specs, check_vma=False
    )
```

```python
import functools

import jax
import jax.numpy as jnp
from jax import lax
from jax.experimental import pallas as pl
from jax.experimental.pallas import tpu as pltpu
from jax.sharding import PartitionSpec as P

DH = 32


EPSILON = 1e-05


def normalize(pair, gain):
    values = pair.astype(jnp.float32)
    center = jnp.mean(values, axis=-1, keepdims=True)
    spread = jnp.mean(jnp.square(values - center), axis=-1, keepdims=True)
    inv_std = lax.rsqrt(spread + EPSILON)
    normed = (values - center) * inv_std
    return ((normed * gain).astype(jnp.bfloat16), normed, inv_std)


def column_grad(tokens, grads, w_qkvg, w_out, bias, scale):
    width = w_out.shape[0]
    heads = bias.shape[0]
    size = width // heads
    count = tokens.shape[0]
    proj = jnp.dot(tokens, w_qkvg, preferred_element_type=jnp.float32)
    queries = proj[:, :width].astype(jnp.bfloat16).reshape(count, heads, size)
    keys = proj[:, width : 2 * width].astype(jnp.bfloat16).reshape(count, heads, size)
    values = proj[:, 2 * width : 3 * width].astype(jnp.bfloat16).reshape(count, heads, size)
    gate = jax.nn.sigmoid(proj[:, 3 * width :]).reshape(count, heads, size)
    scores = jnp.einsum("khd,ihd->hki", keys, queries, preferred_element_type=jnp.float32) * scale
    scores = scores + bias.astype(jnp.float32)
    probs = jax.nn.softmax(scores, axis=1)
    probs_b = probs.astype(jnp.bfloat16)
    attended = jnp.einsum("hki,khd->ihd", probs_b, values, preferred_element_type=jnp.float32)
    mixed = (gate * attended).astype(jnp.bfloat16).reshape(count, width)
    d_mixed = lax.dot_general(
        grads, w_out, (((1,), (1,)), ((), ())), preferred_element_type=jnp.float32
    ).reshape(count, heads, size)
    part_wout = lax.dot_general(
        mixed, grads, (((0,), (0,)), ((), ())), preferred_element_type=jnp.float32
    )
    d_gate = d_mixed * attended * gate * (1.0 - gate)
    d_att = (d_mixed * gate).astype(jnp.bfloat16)
    d_values = jnp.einsum("hki,ihd->khd", probs_b, d_att, preferred_element_type=jnp.float32)
    d_probs = jnp.einsum("ihd,khd->hki", d_att, values, preferred_element_type=jnp.float32)
    delta = jnp.sum(d_att.astype(jnp.float32) * attended, axis=-1)
    d_scores = (probs * (d_probs - delta.T[:, None, :])).astype(jnp.bfloat16)
    d_queries = (
        jnp.einsum("hki,khd->ihd", d_scores, keys, preferred_element_type=jnp.float32) * scale
    )
    d_keys = (
        jnp.einsum("hki,ihd->khd", d_scores, queries, preferred_element_type=jnp.float32) * scale
    )
    d_proj = jnp.concatenate(
        [
            d_queries.reshape(count, width),
            d_keys.reshape(count, width),
            d_values.reshape(count, width),
            d_gate.reshape(count, width),
        ],
        axis=1,
    ).astype(jnp.bfloat16)
    part_qkvg = lax.dot_general(
        tokens, d_proj, (((0,), (0,)), ((), ())), preferred_element_type=jnp.float32
    )
    d_tokens = lax.dot_general(
        d_proj, w_qkvg, (((1,), (1,)), ((), ())), preferred_element_type=jnp.float32
    ).astype(jnp.bfloat16)
    return (d_tokens, d_scores, part_qkvg, part_wout, queries, keys, values, d_att, delta)


def sharded_plan(pair, out_grad, w_qkvg, w_out, w_bias, gain):
    normed_b, normed, inv_std = normalize(pair, gain)
    width = w_out.shape[0]
    heads = w_bias.shape[1]
    scale = DH ** (-0.5)
    columns = lax.all_to_all(normed_b, "row", split_axis=1, concat_axis=0, tiled=True)
    wide_bias = w_bias.astype(jnp.float32)
    local_bias = jnp.einsum(
        "abc,ch->hab", normed_b, w_bias, preferred_element_type=jnp.float32
    ).astype(jnp.bfloat16)
    bias = lax.all_gather(local_bias, "row", axis=1, tiled=True)
    length = bias.shape[1]
    inv_count = 1.0 / length
    inputs = (jnp.swapaxes(columns, 0, 1), jnp.swapaxes(out_grad, 0, 1))

    def step(carry, pieces):
        d_bias, d_qkvg, d_wout = carry
        outs = column_grad(pieces[0], pieces[1], w_qkvg, w_out, bias, scale)
        return ((d_bias + outs[1].astype(jnp.float32), d_qkvg + outs[2], d_wout + outs[3]), outs[0])

    start = (
        jnp.zeros((heads, length, length), jnp.float32),
        jnp.zeros((width, 4 * width), jnp.float32),
        jnp.zeros((width, width), jnp.float32),
    )
    (d_bias, d_qkvg, d_wout), d_cols = lax.scan(step, start, inputs)
    d_att_cols = jnp.swapaxes(d_cols, 0, 1)
    owned = lax.psum_scatter(d_bias, "row", scatter_dimension=1, tiled=True)
    d_att_x = lax.all_to_all(d_att_cols, "row", split_axis=0, concat_axis=1, tiled=True)
    d_bias_x = jnp.einsum("hab,ch->abc", owned, wide_bias, precision=lax.Precision.HIGHEST).astype(
        jnp.bfloat16
    )
    d_wbias = jnp.einsum(
        "abc,hab->ch", normed_b.astype(jnp.float32), owned, precision=lax.Precision.HIGHEST
    )
    d_xn = d_att_x.astype(jnp.float32) + d_bias_x.astype(jnp.float32)
    local_gain = jnp.sum(d_xn * normed, axis=(0, 1))
    scaled = d_xn * gain
    d_pair = (
        inv_std
        * (
            scaled
            - jnp.mean(scaled, axis=-1, keepdims=True)
            - normed * jnp.mean(scaled * normed, axis=-1, keepdims=True)
        )
    ).astype(jnp.bfloat16)
    total_qkvg, total_wout, total_wbias, total_gain = lax.psum(
        (d_qkvg, d_wout, d_wbias, local_gain), "row"
    )
    return (
        d_pair,
        total_qkvg * inv_count,
        total_wout * inv_count,
        total_wbias * inv_count,
        total_gain * inv_count,
    )


BLOCK = 128
PIECE = 32
VMEM_LIMIT = 60 * 1024 * 1024
MASKED = -1e30
BF16 = jnp.bfloat16
F32 = jnp.float32


def mm(a, b, dims=(1, 0)):
    return lax.dot_general(
        a, b, (((dims[0],), (dims[1],)), ((), ())), preferred_element_type=F32
    )


def log2(value):
    return value.bit_length() - 1


def whole_crop(
    n,
    local,
    pair_hbm,
    grad_hbm,
    w_qkvg_hbm,
    w_out_hbm,
    w_bias_hbm,
    gain_hbm,
    d_pair_ref,
    d_qkvg_ref,
    d_wout_ref,
    d_wbias_ref,
    d_gain_ref,
    pairs_ref,
    grads_ref,
    w_qkvg_ref,
    w_out_ref,
    w_bias_ref,
    gain_ref,
    d_xn_ref,
    normed_ref,
    inv_ref,
    send_sems,
    recv_sems,
    local_sems,
):
    me = lax.axis_index("row")
    barrier = pltpu.get_barrier_semaphore()
    for offset in range(1, n):
        pl.semaphore_signal(
            barrier,
            inc=1,
            device_id={"row": lax.rem(me + offset, n)},
            device_id_type=pl.DeviceIdType.MESH,
        )
    staged = [
        pltpu.make_async_copy(src, dst, local_sems.at[index])
        for index, (src, dst) in enumerate(
            (
                (pair_hbm, pairs_ref.at[me]),
                (grad_hbm, grads_ref.at[me]),
                (gain_hbm, gain_ref),
                (w_qkvg_hbm, w_qkvg_ref),
                (w_bias_hbm, w_bias_ref),
                (w_out_hbm, w_out_ref),
            )
        )
    ]
    for copy in staged:
        copy.start()
    staged[0].wait()
    staged[1].wait()
    pl.semaphore_wait(barrier, n - 1)
    sent = []
    for kind, dst in enumerate((pairs_ref, grads_ref)):
        for offset in range(1, n):
            copy = pltpu.make_async_remote_copy(
                src_ref=dst.at[me],
                dst_ref=dst.at[me],
                send_sem=send_sems.at[kind, offset],
                recv_sem=recv_sems.at[kind, offset],
                device_id={"row": lax.rem(me + offset, n)},
                device_id_type=pl.DeviceIdType.MESH,
            )
            copy.start()
            sent.append(copy)

    chunk = pairs_ref.shape[1]
    width = pairs_ref.shape[2]
    heads = w_bias_ref.shape[0]
    size = width // heads
    length = chunk // local
    cells = length * length
    scale = size ** (-0.5)
    inv_count = 1.0 / length
    s_local, s_length, s_chunk = log2(local), log2(length), log2(chunk)

    def iota(shape, axis):
        return lax.broadcasted_iota(jnp.int32, shape, axis)

    def row_of(position):
        return (position & (chunk - 1)) >> s_local

    g, r = iota((cells, cells), 0), iota((cells, cells), 1)
    cell = (row_of(g) << s_length) + ((g >> s_chunk) << s_local) + (g & (local - 1))
    permute = (cell == r).astype(F32).astype(BF16)
    p, q = iota((BLOCK, BLOCK), 0), iota((BLOCK, BLOCK), 1)
    same_column = ((p >> s_chunk) == (q >> s_chunk)) & (((p ^ q) & (local - 1)) == 0)
    p, r = iota((BLOCK, cells), 0), iota((BLOCK, cells), 1)
    spread_key = (row_of(p) == (r >> s_length)).astype(F32).astype(BF16)
    r, p = iota((cells, BLOCK), 0), iota((cells, BLOCK), 1)
    pick_key = (row_of(p) == (r >> s_length)).astype(F32).astype(BF16)
    pick_query = row_of(p) == (r & (length - 1))
    lane_head = iota((BLOCK, width), 1) >> log2(size)

    def per_head(block):
        zero = jnp.zeros_like(block)
        return jnp.concatenate([jnp.where(lane_head == h, block, zero) for h in range(heads)], 0)

    def own_head(stacked):
        out = stacked[:BLOCK]
        for h in range(1, heads):
            out = jnp.where(lane_head == h, stacked[h * BLOCK : (h + 1) * BLOCK], out)
        return out

    for copy in staged[2:5]:
        copy.wait()
    for copy in sent[: n - 1]:
        copy.wait_recv()

    w_bias = w_bias_ref[...]
    w_bias_rows = jnp.concatenate(
        [jnp.broadcast_to(w_bias[h : h + 1], (BLOCK, width)) for h in range(heads)], 0
    ).astype(BF16)
    w_qkvg = w_qkvg_ref[...]
    gain = gain_ref[...]

    values = pairs_ref[...].reshape(cells, width).astype(F32)
    center = jnp.mean(values, axis=-1, keepdims=True)
    spread = jnp.mean(jnp.square(values - center), axis=-1, keepdims=True)
    inv_std = lax.rsqrt(spread + EPSILON)
    normed = (values - center) * inv_std
    xn = (normed * gain).astype(BF16)
    normed_ref[...] = normed
    inv_ref[...] = jnp.broadcast_to(inv_std, (cells, width))

    tokens = mm(permute, xn).astype(BF16)
    proj = mm(tokens, w_qkvg)
    bias_cells = mm(xn, w_bias_rows, (1, 1))
    bias = mm(
        spread_key,
        jnp.concatenate(
            [
                jnp.where(pick_query, bias_cells[:, h * BLOCK : (h + 1) * BLOCK], 0.0)
                for h in range(heads)
            ],
            1,
        ).astype(BF16),
    )
    bias = jnp.concatenate(
        [
            jnp.where(same_column, bias[:, h * BLOCK : (h + 1) * BLOCK], MASKED)
            for h in range(heads)
        ],
        0,
    )
    forward = []
    for start in range(0, cells, BLOCK):
        rows = slice(start, start + BLOCK)
        queries = proj[rows, :width].astype(BF16)
        keys = per_head(proj[rows, width : 2 * width]).astype(BF16)
        vals = per_head(proj[rows, 2 * width : 3 * width]).astype(BF16)
        gate = jax.nn.sigmoid(proj[rows, 3 * width :])
        scores = mm(keys, queries, (1, 1)) * scale + bias
        scores = scores.reshape(heads, BLOCK, BLOCK)
        top = jnp.max(scores, axis=1, keepdims=True)
        weights = jnp.exp(scores - top)
        probs = weights / jnp.sum(weights, axis=1, keepdims=True)
        probs_b = probs.astype(BF16)
        flat_b = probs_b.reshape(heads * BLOCK, BLOCK)
        attended = mm(flat_b, vals, (0, 0))
        forward.append((queries, keys, vals, gate, probs, probs_b, attended))

    for copy in staged[5:]:
        copy.wait()
    for copy in sent[n - 1 :]:
        copy.wait_recv()
    grads = grads_ref[...].reshape(cells, width)
    d_mixed_all = mm(grads, w_out_ref[...], (1, 1))

    mixed_parts, d_proj_parts = [], []
    d_bias_x = jnp.zeros((cells, width), F32)
    d_wbias = jnp.zeros((heads * BLOCK, width), F32)
    for start in range(0, cells, BLOCK):
        queries, keys, vals, gate, probs, probs_b, attended = forward[start // BLOCK]
        rows = slice(start, start + BLOCK)
        flat_b = probs_b.reshape(heads * BLOCK, BLOCK)
        d_mixed = d_mixed_all[rows]
        mixed_parts.append((gate * attended).astype(BF16))
        d_gate = d_mixed * attended * gate * (1.0 - gate)
        d_att = (d_mixed * gate).astype(BF16)
        d_values = own_head(mm(flat_b, d_att))
        d_probs = mm(vals, d_att, (1, 1)).reshape(heads, BLOCK, BLOCK)
        delta = jnp.sum(probs_b.astype(F32) * d_probs, axis=1, keepdims=True)
        d_scores = (probs * (d_probs - delta)).astype(BF16)
        flat_d = d_scores.reshape(heads * BLOCK, BLOCK)
        d_queries = mm(flat_d, keys, (0, 0)) * scale
        d_keys = own_head(mm(flat_d, queries)) * scale
        d_proj_parts.append(
            jnp.concatenate([d_queries, d_keys, d_values, d_gate], 1).astype(BF16)
        )
        terms = mm(pick_key, jnp.concatenate([d_scores[h] for h in range(heads)], 1))
        terms = jnp.concatenate(
            [
                jnp.where(pick_query, terms[:, h * BLOCK : (h + 1) * BLOCK], 0.0)
                for h in range(heads)
            ],
            1,
        ).astype(BF16)
        d_bias_x = d_bias_x + mm(terms, w_bias_rows)
        d_wbias = d_wbias + mm(terms, xn, (0, 0))

    d_proj = jnp.concatenate(d_proj_parts, 0)
    mixed = jnp.concatenate(mixed_parts, 0)
    d_qkvg_ref[...] = mm(tokens, d_proj, (0, 0)) * inv_count
    d_wout_ref[...] = mm(mixed, grads, (0, 0)) * inv_count
    d_wbias_ref[...] = jnp.sum(d_wbias.reshape(heads, BLOCK, width), axis=1) * inv_count
    d_tokens = mm(d_proj, w_qkvg, (1, 1)).astype(BF16)
    d_xn = mm(permute, d_tokens, (0, 0)) + d_bias_x.astype(BF16).astype(F32)
    d_gain_ref[...] = jnp.sum(d_xn * normed, axis=0, keepdims=True) * inv_count
    d_xn_ref[...] = d_xn

    own = pl.ds(pl.multiple_of(me * chunk, chunk), chunk)
    normed = normed_ref[own, :]
    scaled = d_xn_ref[own, :] * gain
    d_pair = inv_ref[own, :] * (
        scaled
        - jnp.mean(scaled, axis=-1, keepdims=True)
        - normed * jnp.mean(scaled * normed, axis=-1, keepdims=True)
    )
    d_pair_ref[...] = d_pair.astype(BF16).reshape(d_pair_ref.shape)
    for copy in sent:
        copy.wait_send()


def deliver(count, *refs):
    ins, outs, held = refs[:count], refs[count : 2 * count], refs[2 * count : 3 * count]
    in_sems, out_sems = refs[3 * count :]
    pieces = []
    for index in range(count):
        rows = ins[index].shape[0]
        step = min(rows, PIECE)
        pieces += [(index, pl.ds(start, step)) for start in range(0, rows, step)]
    loads = [
        pltpu.make_async_copy(ins[index].at[rows], held[index].at[rows], in_sems.at[piece])
        for piece, (index, rows) in enumerate(pieces)
    ]
    stores = [
        pltpu.make_async_copy(held[index].at[rows], outs[index].at[rows], out_sems.at[piece])
        for piece, (index, rows) in enumerate(pieces)
    ]
    for load in loads:
        load.start()
    for load, store in zip(loads, stores):
        load.wait()
        store.start()
    for store in stores:
        store.wait()


def gathered_plan(n, pair, out_grad, w_qkvg, w_out, w_bias, gain):
    local, length, width = pair.shape
    heads = w_bias.shape[1]
    cells = length * length
    chunk = local * length
    vmem = pl.BlockSpec(memory_space=pltpu.VMEM)
    hbm = pl.BlockSpec(memory_space=pltpu.HBM)
    anywhere = pl.BlockSpec(memory_space=pl.ANY)
    shapes = [
        jax.ShapeDtypeStruct(pair.shape, BF16),
        jax.ShapeDtypeStruct(w_qkvg.shape, F32),
        jax.ShapeDtypeStruct(w_out.shape, F32),
        jax.ShapeDtypeStruct((heads, width), F32),
        jax.ShapeDtypeStruct((1, width), F32),
    ]
    results = pl.pallas_call(
        functools.partial(whole_crop, n, local),
        out_shape=shapes,
        in_specs=[hbm] * 6,
        out_specs=[vmem] * 5,
        scratch_shapes=[
            pltpu.VMEM((n, chunk, width), BF16),
            pltpu.VMEM((n, chunk, width), BF16),
            pltpu.VMEM(w_qkvg.shape, BF16),
            pltpu.VMEM(w_out.shape, BF16),
            pltpu.VMEM((heads, width), BF16),
            pltpu.VMEM((1, width), F32),
            pltpu.VMEM((cells, width), F32),
            pltpu.VMEM((cells, width), F32),
            pltpu.VMEM((cells, width), F32),
            pltpu.SemaphoreType.DMA((2, n)),
            pltpu.SemaphoreType.DMA((2, n)),
            pltpu.SemaphoreType.DMA((6,)),
        ],
        compiler_params=pltpu.CompilerParams(
            collective_id=0, has_side_effects=True, vmem_limit_bytes=VMEM_LIMIT
        ),
    )(
        pair.reshape(chunk, width),
        out_grad.reshape(chunk, width),
        w_qkvg,
        w_out,
        w_bias.T,
        gain.reshape(1, width),
    )
    pieces = sum(-(-shape.shape[0] // PIECE) for shape in shapes)
    results = pl.pallas_call(
        functools.partial(deliver, len(shapes)),
        out_shape=shapes,
        in_specs=[anywhere] * len(shapes),
        out_specs=[hbm] * len(shapes),
        scratch_shapes=[pltpu.VMEM(shape.shape, shape.dtype) for shape in shapes]
        + [pltpu.SemaphoreType.DMA((pieces,))] * 2,
        compiler_params=pltpu.CompilerParams(vmem_limit_bytes=VMEM_LIMIT),
    )(*results)
    d_pair, d_qkvg, d_wout, d_wbias, d_gain = results
    return (d_pair, d_qkvg, d_wout, d_wbias.T, d_gain.reshape(width))


def per_device(n, pair, out_grad, w_qkvg, w_out, w_bias, gain):
    local, length, width = pair.shape
    chunk = local * length
    powers = all(size & (size - 1) == 0 for size in (local, length, width, w_bias.shape[1]))
    fits = n > 1 and width == BLOCK and chunk % 16 == 0 and BLOCK % chunk == 0
    if powers and fits and length * length % BLOCK == 0 and length <= 32:
        return gathered_plan(n, pair, out_grad, w_qkvg, w_out, w_bias, gain)
    return sharded_plan(pair, out_grad, w_qkvg, w_out, w_bias, gain)


def solution(mesh):
    in_specs = (P(("crop", "row"), None, None), P("crop", "row", None), P(), P(), P(), P())
    out_specs = (
        P(("crop", "row"), None, None),
        P("crop", None),
        P("crop", None),
        P("crop", None),
        P("crop"),
    )
    return jax.shard_map(
        functools.partial(per_device, mesh.shape["row"]),
        mesh=mesh,
        in_specs=in_specs, out_specs=out_specs, check_vma=False
    )
```

```python
import functools

import jax
import jax.numpy as jnp
from jax import lax
from jax.experimental import pallas as pl
from jax.experimental.pallas import tpu as pltpu
from jax.sharding import PartitionSpec as P

DH = 32


EPSILON = 1e-05


def normalize(pair, gain):
    values = pair.astype(jnp.float32)
    center = jnp.mean(values, axis=-1, keepdims=True)
    spread = jnp.mean(jnp.square(values - center), axis=-1, keepdims=True)
    inv_std = lax.rsqrt(spread + EPSILON)
    normed = (values - center) * inv_std
    return ((normed * gain).astype(jnp.bfloat16), normed, inv_std)


def column_grad(tokens, grads, w_qkvg, w_out, bias, scale):
    width = w_out.shape[0]
    heads = bias.shape[0]
    size = width // heads
    count = tokens.shape[0]
    proj = jnp.dot(tokens, w_qkvg, preferred_element_type=jnp.float32)
    queries = proj[:, :width].astype(jnp.bfloat16).reshape(count, heads, size)
    keys = proj[:, width : 2 * width].astype(jnp.bfloat16).reshape(count, heads, size)
    values = proj[:, 2 * width : 3 * width].astype(jnp.bfloat16).reshape(count, heads, size)
    gate = jax.nn.sigmoid(proj[:, 3 * width :]).reshape(count, heads, size)
    scores = jnp.einsum("khd,ihd->hki", keys, queries, preferred_element_type=jnp.float32) * scale
    scores = scores + bias.astype(jnp.float32)
    probs = jax.nn.softmax(scores, axis=1)
    probs_b = probs.astype(jnp.bfloat16)
    attended = jnp.einsum("hki,khd->ihd", probs_b, values, preferred_element_type=jnp.float32)
    mixed = (gate * attended).astype(jnp.bfloat16).reshape(count, width)
    d_mixed = lax.dot_general(
        grads, w_out, (((1,), (1,)), ((), ())), preferred_element_type=jnp.float32
    ).reshape(count, heads, size)
    part_wout = lax.dot_general(
        mixed, grads, (((0,), (0,)), ((), ())), preferred_element_type=jnp.float32
    )
    d_gate = d_mixed * attended * gate * (1.0 - gate)
    d_att = (d_mixed * gate).astype(jnp.bfloat16)
    d_values = jnp.einsum("hki,ihd->khd", probs_b, d_att, preferred_element_type=jnp.float32)
    d_probs = jnp.einsum("ihd,khd->hki", d_att, values, preferred_element_type=jnp.float32)
    delta = jnp.sum(d_att.astype(jnp.float32) * attended, axis=-1)
    d_scores = (probs * (d_probs - delta.T[:, None, :])).astype(jnp.bfloat16)
    d_queries = (
        jnp.einsum("hki,khd->ihd", d_scores, keys, preferred_element_type=jnp.float32) * scale
    )
    d_keys = (
        jnp.einsum("hki,ihd->khd", d_scores, queries, preferred_element_type=jnp.float32) * scale
    )
    d_proj = jnp.concatenate(
        [
            d_queries.reshape(count, width),
            d_keys.reshape(count, width),
            d_values.reshape(count, width),
            d_gate.reshape(count, width),
        ],
        axis=1,
    ).astype(jnp.bfloat16)
    part_qkvg = lax.dot_general(
        tokens, d_proj, (((0,), (0,)), ((), ())), preferred_element_type=jnp.float32
    )
    d_tokens = lax.dot_general(
        d_proj, w_qkvg, (((1,), (1,)), ((), ())), preferred_element_type=jnp.float32
    ).astype(jnp.bfloat16)
    return (d_tokens, d_scores, part_qkvg, part_wout, queries, keys, values, d_att, delta)


def sharded_plan(pair, out_grad, w_qkvg, w_out, w_bias, gain):
    normed_b, normed, inv_std = normalize(pair, gain)
    width = w_out.shape[0]
    heads = w_bias.shape[1]
    scale = DH ** (-0.5)
    columns = lax.all_to_all(normed_b, "row", split_axis=1, concat_axis=0, tiled=True)
    wide_bias = w_bias.astype(jnp.float32)
    local_bias = jnp.einsum(
        "abc,ch->hab", normed_b, w_bias, preferred_element_type=jnp.float32
    ).astype(jnp.bfloat16)
    bias = lax.all_gather(local_bias, "row", axis=1, tiled=True)
    length = bias.shape[1]
    inv_count = 1.0 / length
    inputs = (jnp.swapaxes(columns, 0, 1), jnp.swapaxes(out_grad, 0, 1))

    def step(carry, pieces):
        d_bias, d_qkvg, d_wout = carry
        outs = column_grad(pieces[0], pieces[1], w_qkvg, w_out, bias, scale)
        return ((d_bias + outs[1].astype(jnp.float32), d_qkvg + outs[2], d_wout + outs[3]), outs[0])

    start = (
        jnp.zeros((heads, length, length), jnp.float32),
        jnp.zeros((width, 4 * width), jnp.float32),
        jnp.zeros((width, width), jnp.float32),
    )
    (d_bias, d_qkvg, d_wout), d_cols = lax.scan(step, start, inputs)
    d_att_cols = jnp.swapaxes(d_cols, 0, 1)
    owned = lax.psum_scatter(d_bias, "row", scatter_dimension=1, tiled=True)
    d_att_x = lax.all_to_all(d_att_cols, "row", split_axis=0, concat_axis=1, tiled=True)
    d_bias_x = jnp.einsum("hab,ch->abc", owned, wide_bias, precision=lax.Precision.HIGHEST).astype(
        jnp.bfloat16
    )
    d_wbias = jnp.einsum(
        "abc,hab->ch", normed_b.astype(jnp.float32), owned, precision=lax.Precision.HIGHEST
    )
    d_xn = d_att_x.astype(jnp.float32) + d_bias_x.astype(jnp.float32)
    local_gain = jnp.sum(d_xn * normed, axis=(0, 1))
    scaled = d_xn * gain
    d_pair = (
        inv_std
        * (
            scaled
            - jnp.mean(scaled, axis=-1, keepdims=True)
            - normed * jnp.mean(scaled * normed, axis=-1, keepdims=True)
        )
    ).astype(jnp.bfloat16)
    total_qkvg, total_wout, total_wbias, total_gain = lax.psum(
        (d_qkvg, d_wout, d_wbias, local_gain), "row"
    )
    return (
        d_pair,
        total_qkvg * inv_count,
        total_wout * inv_count,
        total_wbias * inv_count,
        total_gain * inv_count,
    )


BLOCK = 128
VMEM_LIMIT = 16 * 1024 * 1024
MASKED = -1e30
BF16 = jnp.bfloat16
F32 = jnp.float32


def mm(a, b, dims=(1, 0)):
    return lax.dot_general(
        a, b, (((dims[0],), (dims[1],)), ((), ())), preferred_element_type=F32
    )


def log2(value):
    return value.bit_length() - 1


def whole_crop(
    n,
    local,
    pair_hbm,
    grad_hbm,
    w_qkvg_hbm,
    w_out_hbm,
    w_bias_hbm,
    gain_hbm,
    d_pair_ref,
    d_qkvg_ref,
    d_wout_ref,
    d_wbias_ref,
    d_gain_ref,
    pairs_ref,
    grads_ref,
    w_qkvg_ref,
    w_out_ref,
    w_bias_ref,
    gain_ref,
    d_xn_ref,
    normed_ref,
    inv_ref,
    send_sems,
    recv_sems,
    local_sems,
):
    me = lax.axis_index("row")
    barrier = pltpu.get_barrier_semaphore()
    for offset in range(1, n):
        pl.semaphore_signal(
            barrier,
            inc=1,
            device_id={"row": lax.rem(me + offset, n)},
            device_id_type=pl.DeviceIdType.MESH,
        )
    staged = [
        pltpu.make_async_copy(src, dst, local_sems.at[index])
        for index, (src, dst) in enumerate(
            (
                (pair_hbm, pairs_ref.at[me]),
                (grad_hbm, grads_ref.at[me]),
                (gain_hbm, gain_ref),
                (w_qkvg_hbm, w_qkvg_ref),
                (w_bias_hbm, w_bias_ref),
                (w_out_hbm, w_out_ref),
            )
        )
    ]
    for copy in staged:
        copy.start()
    staged[0].wait()
    staged[1].wait()
    pl.semaphore_wait(barrier, n - 1)
    sent = []
    for kind, dst in enumerate((pairs_ref, grads_ref)):
        for offset in range(1, n):
            copy = pltpu.make_async_remote_copy(
                src_ref=dst.at[me],
                dst_ref=dst.at[me],
                send_sem=send_sems.at[kind, offset],
                recv_sem=recv_sems.at[kind, offset],
                device_id={"row": lax.rem(me + offset, n)},
                device_id_type=pl.DeviceIdType.MESH,
            )
            copy.start()
            sent.append(copy)

    chunk = pairs_ref.shape[1]
    width = pairs_ref.shape[2]
    heads = w_bias_ref.shape[0]
    size = width // heads
    length = chunk // local
    cells = length * length
    scale = size ** (-0.5)
    inv_count = 1.0 / length
    s_local, s_length, s_chunk = log2(local), log2(length), log2(chunk)

    def iota(shape, axis):
        return lax.broadcasted_iota(jnp.int32, shape, axis)

    def row_of(position):
        return (position & (chunk - 1)) >> s_local

    g, r = iota((cells, cells), 0), iota((cells, cells), 1)
    cell = (row_of(g) << s_length) + ((g >> s_chunk) << s_local) + (g & (local - 1))
    permute = (cell == r).astype(F32).astype(BF16)
    p, q = iota((BLOCK, BLOCK), 0), iota((BLOCK, BLOCK), 1)
    same_column = ((p >> s_chunk) == (q >> s_chunk)) & (((p ^ q) & (local - 1)) == 0)
    p, r = iota((BLOCK, cells), 0), iota((BLOCK, cells), 1)
    spread_key = (row_of(p) == (r >> s_length)).astype(F32).astype(BF16)
    r, p = iota((cells, BLOCK), 0), iota((cells, BLOCK), 1)
    pick_key = (row_of(p) == (r >> s_length)).astype(F32).astype(BF16)
    pick_query = row_of(p) == (r & (length - 1))
    lane_head = iota((BLOCK, width), 1) >> log2(size)

    def per_head(block):
        zero = jnp.zeros_like(block)
        return jnp.concatenate([jnp.where(lane_head == h, block, zero) for h in range(heads)], 0)

    def own_head(stacked):
        out = stacked[:BLOCK]
        for h in range(1, heads):
            out = jnp.where(lane_head == h, stacked[h * BLOCK : (h + 1) * BLOCK], out)
        return out

    for copy in staged[2:5]:
        copy.wait()
    for copy in sent[: n - 1]:
        copy.wait_recv()

    w_bias = w_bias_ref[...]
    w_bias_rows = jnp.concatenate(
        [jnp.broadcast_to(w_bias[h : h + 1], (BLOCK, width)) for h in range(heads)], 0
    ).astype(BF16)
    w_qkvg = w_qkvg_ref[...]
    gain = gain_ref[...]

    values = pairs_ref[...].reshape(cells, width).astype(F32)
    center = jnp.mean(values, axis=-1, keepdims=True)
    spread = jnp.mean(jnp.square(values - center), axis=-1, keepdims=True)
    inv_std = lax.rsqrt(spread + EPSILON)
    normed = (values - center) * inv_std
    xn = (normed * gain).astype(BF16)
    normed_ref[...] = normed
    inv_ref[...] = jnp.broadcast_to(inv_std, (cells, width))

    tokens = mm(permute, xn).astype(BF16)
    proj = mm(tokens, w_qkvg)
    bias_cells = mm(xn, w_bias_rows, (1, 1))
    bias = mm(
        spread_key,
        jnp.concatenate(
            [
                jnp.where(pick_query, bias_cells[:, h * BLOCK : (h + 1) * BLOCK], 0.0)
                for h in range(heads)
            ],
            1,
        ).astype(BF16),
    )
    bias = jnp.concatenate(
        [
            jnp.where(same_column, bias[:, h * BLOCK : (h + 1) * BLOCK], MASKED)
            for h in range(heads)
        ],
        0,
    )
    forward = []
    for start in range(0, cells, BLOCK):
        rows = slice(start, start + BLOCK)
        queries = proj[rows, :width].astype(BF16)
        keys = per_head(proj[rows, width : 2 * width]).astype(BF16)
        vals = per_head(proj[rows, 2 * width : 3 * width]).astype(BF16)
        gate = jax.nn.sigmoid(proj[rows, 3 * width :])
        scores = mm(keys, queries, (1, 1)) * scale + bias
        scores = scores.reshape(heads, BLOCK, BLOCK)
        top = jnp.max(scores, axis=1, keepdims=True)
        weights = jnp.exp(scores - top)
        probs = weights / jnp.sum(weights, axis=1, keepdims=True)
        probs_b = probs.astype(BF16)
        flat_b = probs_b.reshape(heads * BLOCK, BLOCK)
        attended = mm(flat_b, vals, (0, 0))
        forward.append((queries, keys, vals, gate, probs, probs_b, attended))

    for copy in staged[5:]:
        copy.wait()
    for copy in sent[n - 1 :]:
        copy.wait_recv()
    grads = grads_ref[...].reshape(cells, width)
    d_mixed_all = mm(grads, w_out_ref[...], (1, 1))

    mixed_parts, d_proj_parts = [], []
    d_bias_x = jnp.zeros((cells, width), F32)
    d_wbias = jnp.zeros((heads * BLOCK, width), F32)
    for start in range(0, cells, BLOCK):
        queries, keys, vals, gate, probs, probs_b, attended = forward[start // BLOCK]
        rows = slice(start, start + BLOCK)
        flat_b = probs_b.reshape(heads * BLOCK, BLOCK)
        d_mixed = d_mixed_all[rows]
        mixed_parts.append((gate * attended).astype(BF16))
        d_gate = d_mixed * attended * gate * (1.0 - gate)
        d_att = (d_mixed * gate).astype(BF16)
        d_values = own_head(mm(flat_b, d_att))
        d_probs = mm(vals, d_att, (1, 1)).reshape(heads, BLOCK, BLOCK)
        delta = jnp.sum(probs_b.astype(F32) * d_probs, axis=1, keepdims=True)
        d_scores = (probs * (d_probs - delta)).astype(BF16)
        flat_d = d_scores.reshape(heads * BLOCK, BLOCK)
        d_queries = mm(flat_d, keys, (0, 0)) * scale
        d_keys = own_head(mm(flat_d, queries)) * scale
        d_proj_parts.append(
            jnp.concatenate([d_queries, d_keys, d_values, d_gate], 1).astype(BF16)
        )
        terms = mm(pick_key, jnp.concatenate([d_scores[h] for h in range(heads)], 1))
        terms = jnp.concatenate(
            [
                jnp.where(pick_query, terms[:, h * BLOCK : (h + 1) * BLOCK], 0.0)
                for h in range(heads)
            ],
            1,
        ).astype(BF16)
        d_bias_x = d_bias_x + mm(terms, w_bias_rows)
        d_wbias = d_wbias + mm(terms, xn, (0, 0))

    d_proj = jnp.concatenate(d_proj_parts, 0)
    mixed = jnp.concatenate(mixed_parts, 0)
    d_qkvg_ref[...] = mm(tokens, d_proj, (0, 0)) * inv_count
    d_wout_ref[...] = mm(mixed, grads, (0, 0)) * inv_count
    d_wbias_ref[...] = jnp.sum(d_wbias.reshape(heads, BLOCK, width), axis=1) * inv_count
    d_tokens = mm(d_proj, w_qkvg, (1, 1)).astype(BF16)
    d_xn = mm(permute, d_tokens, (0, 0)) + d_bias_x.astype(BF16).astype(F32)
    d_gain_ref[...] = jnp.sum(d_xn * normed, axis=0, keepdims=True) * inv_count
    d_xn_ref[...] = d_xn

    own = pl.ds(pl.multiple_of(me * chunk, chunk), chunk)
    normed = normed_ref[own, :]
    scaled = d_xn_ref[own, :] * gain
    d_pair = inv_ref[own, :] * (
        scaled
        - jnp.mean(scaled, axis=-1, keepdims=True)
        - normed * jnp.mean(scaled * normed, axis=-1, keepdims=True)
    )
    d_pair_ref[...] = d_pair.astype(BF16).reshape(d_pair_ref.shape)
    for copy in sent:
        copy.wait_send()


def deliver(count, *refs):
    copies = [
        pltpu.make_async_copy(refs[index], refs[count + index], refs[-1].at[index])
        for index in range(count)
    ]
    for copy in copies:
        copy.start()
    for copy in copies:
        copy.wait()


def gathered_plan(n, pair, out_grad, w_qkvg, w_out, w_bias, gain):
    local, length, width = pair.shape
    heads = w_bias.shape[1]
    cells = length * length
    chunk = local * length
    vmem = pl.BlockSpec(memory_space=pltpu.VMEM)
    hbm = pl.BlockSpec(memory_space=pltpu.HBM)
    shapes = [
        jax.ShapeDtypeStruct(pair.shape, BF16),
        jax.ShapeDtypeStruct(w_qkvg.shape, F32),
        jax.ShapeDtypeStruct(w_out.shape, F32),
        jax.ShapeDtypeStruct((heads, width), F32),
        jax.ShapeDtypeStruct((1, width), F32),
    ]
    operands = (
        pair.reshape(chunk, width),
        out_grad.reshape(chunk, width),
        w_qkvg,
        w_out,
        w_bias.T,
        gain.reshape(1, width),
    )
    results = pl.pallas_call(
        functools.partial(whole_crop, n, local),
        out_shape=[pltpu.VMEM(shape.shape, shape.dtype) for shape in shapes],
        in_specs=[hbm] * 6,
        out_specs=[vmem] * 5,
        scratch_shapes=[
            pltpu.VMEM((n, chunk, width), BF16),
            pltpu.VMEM((n, chunk, width), BF16),
            pltpu.VMEM(w_qkvg.shape, BF16),
            pltpu.VMEM(w_out.shape, BF16),
            pltpu.VMEM((heads, width), BF16),
            pltpu.VMEM((1, width), F32),
            pltpu.VMEM((cells, width), F32),
            pltpu.VMEM((cells, width), F32),
            pltpu.VMEM((cells, width), F32),
            pltpu.SemaphoreType.DMA((2, n)),
            pltpu.SemaphoreType.DMA((2, n)),
            pltpu.SemaphoreType.DMA((6,)),
        ],
        compiler_params=pltpu.CompilerParams(
            collective_id=0, has_side_effects=True, vmem_limit_bytes=VMEM_LIMIT
        ),
    )(*[pltpu.with_memory_space_constraint(value, pltpu.HBM) for value in operands])
    results = pl.pallas_call(
        functools.partial(deliver, len(shapes)),
        out_shape=shapes,
        in_specs=[vmem] * len(shapes),
        out_specs=[hbm] * len(shapes),
        scratch_shapes=[pltpu.SemaphoreType.DMA((len(shapes),))],
        compiler_params=pltpu.CompilerParams(vmem_limit_bytes=VMEM_LIMIT),
    )(*results)
    d_pair, d_qkvg, d_wout, d_wbias, d_gain = results
    return (d_pair, d_qkvg, d_wout, d_wbias.T, d_gain.reshape(width))


def per_device(n, pair, out_grad, w_qkvg, w_out, w_bias, gain):
    local, length, width = pair.shape
    chunk = local * length
    powers = all(size & (size - 1) == 0 for size in (local, length, width, w_bias.shape[1]))
    fits = n > 1 and width == BLOCK and chunk % 16 == 0 and BLOCK % chunk == 0
    if powers and fits and length * length % BLOCK == 0 and length <= 32:
        return gathered_plan(n, pair, out_grad, w_qkvg, w_out, w_bias, gain)
    return sharded_plan(pair, out_grad, w_qkvg, w_out, w_bias, gain)


def solution(mesh):
    in_specs = (P(("crop", "row"), None, None), P("crop", "row", None), P(), P(), P(), P())
    out_specs = (
        P(("crop", "row"), None, None),
        P("crop", None),
        P("crop", None),
        P("crop", None),
        P("crop"),
    )
    return jax.shard_map(
        functools.partial(per_device, mesh.shape["row"]),
        mesh=mesh,
        in_specs=in_specs, out_specs=out_specs, check_vma=False
    )
```

```python
import functools

import jax
import jax.numpy as jnp
from jax import lax
from jax.experimental import pallas as pl
from jax.experimental.pallas import tpu as pltpu
from jax.sharding import PartitionSpec as P

DH = 32


EPSILON = 1e-05


def normalize(pair, gain):
    values = pair.astype(jnp.float32)
    center = jnp.mean(values, axis=-1, keepdims=True)
    spread = jnp.mean(jnp.square(values - center), axis=-1, keepdims=True)
    inv_std = lax.rsqrt(spread + EPSILON)
    normed = (values - center) * inv_std
    return ((normed * gain).astype(jnp.bfloat16), normed, inv_std)


def column_grad(tokens, grads, w_qkvg, w_out, bias, scale):
    width = w_out.shape[0]
    heads = bias.shape[0]
    size = width // heads
    count = tokens.shape[0]
    proj = jnp.dot(tokens, w_qkvg, preferred_element_type=jnp.float32)
    queries = proj[:, :width].astype(jnp.bfloat16).reshape(count, heads, size)
    keys = proj[:, width : 2 * width].astype(jnp.bfloat16).reshape(count, heads, size)
    values = proj[:, 2 * width : 3 * width].astype(jnp.bfloat16).reshape(count, heads, size)
    gate = jax.nn.sigmoid(proj[:, 3 * width :]).reshape(count, heads, size)
    scores = jnp.einsum("khd,ihd->hki", keys, queries, preferred_element_type=jnp.float32) * scale
    scores = scores + bias.astype(jnp.float32)
    probs = jax.nn.softmax(scores, axis=1)
    probs_b = probs.astype(jnp.bfloat16)
    attended = jnp.einsum("hki,khd->ihd", probs_b, values, preferred_element_type=jnp.float32)
    mixed = (gate * attended).astype(jnp.bfloat16).reshape(count, width)
    d_mixed = lax.dot_general(
        grads, w_out, (((1,), (1,)), ((), ())), preferred_element_type=jnp.float32
    ).reshape(count, heads, size)
    part_wout = lax.dot_general(
        mixed, grads, (((0,), (0,)), ((), ())), preferred_element_type=jnp.float32
    )
    d_gate = d_mixed * attended * gate * (1.0 - gate)
    d_att = (d_mixed * gate).astype(jnp.bfloat16)
    d_values = jnp.einsum("hki,ihd->khd", probs_b, d_att, preferred_element_type=jnp.float32)
    d_probs = jnp.einsum("ihd,khd->hki", d_att, values, preferred_element_type=jnp.float32)
    delta = jnp.sum(d_att.astype(jnp.float32) * attended, axis=-1)
    d_scores = (probs * (d_probs - delta.T[:, None, :])).astype(jnp.bfloat16)
    d_queries = (
        jnp.einsum("hki,khd->ihd", d_scores, keys, preferred_element_type=jnp.float32) * scale
    )
    d_keys = (
        jnp.einsum("hki,ihd->khd", d_scores, queries, preferred_element_type=jnp.float32) * scale
    )
    d_proj = jnp.concatenate(
        [
            d_queries.reshape(count, width),
            d_keys.reshape(count, width),
            d_values.reshape(count, width),
            d_gate.reshape(count, width),
        ],
        axis=1,
    ).astype(jnp.bfloat16)
    part_qkvg = lax.dot_general(
        tokens, d_proj, (((0,), (0,)), ((), ())), preferred_element_type=jnp.float32
    )
    d_tokens = lax.dot_general(
        d_proj, w_qkvg, (((1,), (1,)), ((), ())), preferred_element_type=jnp.float32
    ).astype(jnp.bfloat16)
    return (d_tokens, d_scores, part_qkvg, part_wout, queries, keys, values, d_att, delta)


def sharded_plan(pair, out_grad, w_qkvg, w_out, w_bias, gain):
    normed_b, normed, inv_std = normalize(pair, gain)
    width = w_out.shape[0]
    heads = w_bias.shape[1]
    scale = DH ** (-0.5)
    columns = lax.all_to_all(normed_b, "row", split_axis=1, concat_axis=0, tiled=True)
    wide_bias = w_bias.astype(jnp.float32)
    local_bias = jnp.einsum(
        "abc,ch->hab", normed_b, w_bias, preferred_element_type=jnp.float32
    ).astype(jnp.bfloat16)
    bias = lax.all_gather(local_bias, "row", axis=1, tiled=True)
    length = bias.shape[1]
    inv_count = 1.0 / length
    inputs = (jnp.swapaxes(columns, 0, 1), jnp.swapaxes(out_grad, 0, 1))

    def step(carry, pieces):
        d_bias, d_qkvg, d_wout = carry
        outs = column_grad(pieces[0], pieces[1], w_qkvg, w_out, bias, scale)
        return ((d_bias + outs[1].astype(jnp.float32), d_qkvg + outs[2], d_wout + outs[3]), outs[0])

    start = (
        jnp.zeros((heads, length, length), jnp.float32),
        jnp.zeros((width, 4 * width), jnp.float32),
        jnp.zeros((width, width), jnp.float32),
    )
    (d_bias, d_qkvg, d_wout), d_cols = lax.scan(step, start, inputs)
    d_att_cols = jnp.swapaxes(d_cols, 0, 1)
    owned = lax.psum_scatter(d_bias, "row", scatter_dimension=1, tiled=True)
    d_att_x = lax.all_to_all(d_att_cols, "row", split_axis=0, concat_axis=1, tiled=True)
    d_bias_x = jnp.einsum("hab,ch->abc", owned, wide_bias, precision=lax.Precision.HIGHEST).astype(
        jnp.bfloat16
    )
    d_wbias = jnp.einsum(
        "abc,hab->ch", normed_b.astype(jnp.float32), owned, precision=lax.Precision.HIGHEST
    )
    d_xn = d_att_x.astype(jnp.float32) + d_bias_x.astype(jnp.float32)
    local_gain = jnp.sum(d_xn * normed, axis=(0, 1))
    scaled = d_xn * gain
    d_pair = (
        inv_std
        * (
            scaled
            - jnp.mean(scaled, axis=-1, keepdims=True)
            - normed * jnp.mean(scaled * normed, axis=-1, keepdims=True)
        )
    ).astype(jnp.bfloat16)
    total_qkvg, total_wout, total_wbias, total_gain = lax.psum(
        (d_qkvg, d_wout, d_wbias, local_gain), "row"
    )
    return (
        d_pair,
        total_qkvg * inv_count,
        total_wout * inv_count,
        total_wbias * inv_count,
        total_gain * inv_count,
    )


BLOCK = 128
VMEM_LIMIT = 16 * 1024 * 1024
MASKED = -1e30
BF16 = jnp.bfloat16
F32 = jnp.float32


def mm(a, b, dims=(1, 0)):
    return lax.dot_general(
        a, b, (((dims[0],), (dims[1],)), ((), ())), preferred_element_type=F32
    )


def log2(value):
    return value.bit_length() - 1


def partner(me, step):
    other = me
    for bit in range(log2(step) + 1):
        weight = 1 << bit
        if step & weight:
            other = other + weight * (1 - 2 * lax.rem(me // weight, 2))
    return other


def whole_crop(
    n,
    local,
    pair_hbm,
    grad_hbm,
    w_qkvg_hbm,
    w_out_hbm,
    w_bias_hbm,
    gain_hbm,
    tokens_ref,
    d_proj_ref,
    mixed_ref,
    grads_ref,
    d_bias_x_ref,
    normed_ref,
    inv_ref,
    w_qkvg_ref,
    gain_ref,
    restore_ref,
    d_wbias_ref,
    pairs_ref,
    w_out_ref,
    w_bias_ref,
    send_sems,
    recv_sems,
    local_sems,
):
    me = lax.axis_index("row")
    partners = {step: partner(me, step) for step in range(1, n)}
    barrier = pltpu.get_barrier_semaphore()
    for step in partners:
        pl.semaphore_signal(
            barrier,
            inc=1,
            device_id={"row": partners[step]},
            device_id_type=pl.DeviceIdType.MESH,
        )
    staged = [
        pltpu.make_async_copy(src, dst, local_sems.at[index])
        for index, (src, dst) in enumerate(
            (
                (pair_hbm, pairs_ref.at[me]),
                (grad_hbm, grads_ref.at[me]),
                (gain_hbm, gain_ref),
                (w_qkvg_hbm, w_qkvg_ref),
                (w_bias_hbm, w_bias_ref),
                (w_out_hbm, w_out_ref),
            )
        )
    ]
    for copy in staged:
        copy.start()
    staged[0].wait()
    staged[1].wait()
    pl.semaphore_wait(barrier, n - 1)
    sent = []
    for kind, dst in enumerate((pairs_ref, grads_ref)):
        for step in reversed(range(1, n)):
            copy = pltpu.make_async_remote_copy(
                src_ref=dst.at[me],
                dst_ref=dst.at[me],
                send_sem=send_sems.at[kind, step],
                recv_sem=recv_sems.at[kind, step],
                device_id={"row": partners[step]},
                device_id_type=pl.DeviceIdType.MESH,
            )
            copy.start()
            sent.append(copy)

    chunk = pairs_ref.shape[1]
    width = pairs_ref.shape[2]
    heads = w_bias_ref.shape[0]
    size = width // heads
    length = chunk // local
    cells = length * length
    scale = size ** (-0.5)
    inv_count = 1.0 / length
    s_local, s_length, s_chunk = log2(local), log2(length), log2(chunk)

    def iota(shape, axis):
        return lax.broadcasted_iota(jnp.int32, shape, axis)

    def row_of(position):
        return (position & (chunk - 1)) >> s_local

    g, r = iota((cells, cells), 0), iota((cells, cells), 1)
    cell = (row_of(g) << s_length) + ((g >> s_chunk) << s_local) + (g & (local - 1))
    permute = (cell == r).astype(F32).astype(BF16)
    r, g = iota((cells, cells), 0), iota((cells, cells), 1)
    cell = (row_of(g) << s_length) + ((g >> s_chunk) << s_local) + (g & (local - 1))
    restore_ref[...] = (cell == r).astype(F32).astype(BF16)
    p, q = iota((BLOCK, BLOCK), 0), iota((BLOCK, BLOCK), 1)
    same_column = ((p >> s_chunk) == (q >> s_chunk)) & (((p ^ q) & (local - 1)) == 0)
    p, r = iota((BLOCK, cells), 0), iota((BLOCK, cells), 1)
    spread_key = (row_of(p) == (r >> s_length)).astype(F32).astype(BF16)
    r, p = iota((cells, BLOCK), 0), iota((cells, BLOCK), 1)
    pick_key = (row_of(p) == (r >> s_length)).astype(F32).astype(BF16)
    pick_query = row_of(p) == (r & (length - 1))
    lane_head = iota((BLOCK, width), 1) >> log2(size)

    def per_head(block):
        zero = jnp.zeros_like(block)
        return jnp.concatenate([jnp.where(lane_head == h, block, zero) for h in range(heads)], 0)

    def own_head(stacked):
        out = stacked[:BLOCK]
        for h in range(1, heads):
            out = jnp.where(lane_head == h, stacked[h * BLOCK : (h + 1) * BLOCK], out)
        return out

    for copy in staged[2:5]:
        copy.wait()
    for copy in sent[: n - 1]:
        copy.wait_recv()

    w_bias = w_bias_ref[...]
    w_bias_rows = jnp.concatenate(
        [jnp.broadcast_to(w_bias[h : h + 1], (BLOCK, width)) for h in range(heads)], 0
    ).astype(BF16)
    w_qkvg = w_qkvg_ref[...]
    gain = gain_ref[...]

    values = pairs_ref[...].reshape(cells, width).astype(F32)
    center = jnp.mean(values, axis=-1, keepdims=True)
    spread = jnp.mean(jnp.square(values - center), axis=-1, keepdims=True)
    inv_std = lax.rsqrt(spread + EPSILON)
    normed = (values - center) * inv_std
    xn = (normed * gain).astype(BF16)
    normed_ref[...] = normed
    inv_ref[...] = jnp.broadcast_to(inv_std, (cells, width))

    tokens = mm(permute, xn).astype(BF16)
    tokens_ref[...] = tokens
    proj = mm(tokens, w_qkvg)
    bias_cells = mm(xn, w_bias_rows, (1, 1))
    bias = mm(
        spread_key,
        jnp.concatenate(
            [
                jnp.where(pick_query, bias_cells[:, h * BLOCK : (h + 1) * BLOCK], 0.0)
                for h in range(heads)
            ],
            1,
        ).astype(BF16),
    )
    bias = jnp.concatenate(
        [
            jnp.where(same_column, bias[:, h * BLOCK : (h + 1) * BLOCK], MASKED)
            for h in range(heads)
        ],
        0,
    )
    forward = []
    for start in range(0, cells, BLOCK):
        rows = slice(start, start + BLOCK)
        queries = proj[rows, :width].astype(BF16)
        keys = per_head(proj[rows, width : 2 * width]).astype(BF16)
        vals = per_head(proj[rows, 2 * width : 3 * width]).astype(BF16)
        gate = jax.nn.sigmoid(proj[rows, 3 * width :])
        scores = mm(keys, queries, (1, 1)) * scale + bias
        scores = scores.reshape(heads, BLOCK, BLOCK)
        top = jnp.max(scores, axis=1, keepdims=True)
        weights = jnp.exp(scores - top)
        probs = weights * (1.0 / jnp.sum(weights, axis=1, keepdims=True))
        probs_b = probs.astype(BF16)
        flat_b = probs_b.reshape(heads * BLOCK, BLOCK)
        attended = mm(flat_b, vals, (0, 0))
        forward.append((queries, keys, vals, gate, probs, probs_b, attended))

    for copy in staged[5:]:
        copy.wait()
    for copy in sent[n - 1 :]:
        copy.wait_recv()
    grads = grads_ref[...].reshape(cells, width)
    d_mixed_all = mm(grads, w_out_ref[...], (1, 1))

    d_bias_x = jnp.zeros((cells, width), F32)
    d_wbias = jnp.zeros((heads * BLOCK, width), F32)
    for start in range(0, cells, BLOCK):
        queries, keys, vals, gate, probs, probs_b, attended = forward[start // BLOCK]
        rows = slice(start, start + BLOCK)
        flat_b = probs_b.reshape(heads * BLOCK, BLOCK)
        d_mixed = d_mixed_all[rows]
        mixed_ref[rows, :] = (gate * attended).astype(BF16)
        d_gate = d_mixed * attended * gate * (1.0 - gate)
        d_att = (d_mixed * gate).astype(BF16)
        d_values = own_head(mm(flat_b, d_att))
        d_probs = mm(vals, d_att, (1, 1)).reshape(heads, BLOCK, BLOCK)
        delta = jnp.sum(probs_b.astype(F32) * d_probs, axis=1, keepdims=True)
        d_scores = (probs * (d_probs - delta)).astype(BF16)
        flat_d = d_scores.reshape(heads * BLOCK, BLOCK)
        d_queries = mm(flat_d, keys, (0, 0)) * scale
        d_keys = own_head(mm(flat_d, queries)) * scale
        for index, part in enumerate((d_queries, d_keys, d_values, d_gate)):
            d_proj_ref[rows, index * width : (index + 1) * width] = part.astype(BF16)
        terms = mm(pick_key, jnp.concatenate([d_scores[h] for h in range(heads)], 1))
        terms = jnp.concatenate(
            [
                jnp.where(pick_query, terms[:, h * BLOCK : (h + 1) * BLOCK], 0.0)
                for h in range(heads)
            ],
            1,
        ).astype(BF16)
        d_bias_x = d_bias_x + mm(terms, w_bias_rows)
        d_wbias = d_wbias + mm(terms, xn, (0, 0))

    d_bias_x_ref[...] = d_bias_x.astype(BF16)
    d_wbias_ref[...] = jnp.sum(d_wbias.reshape(heads, BLOCK, width), axis=1) * inv_count
    for copy in sent:
        copy.wait_send()


def finish(
    inv_count,
    tokens_ref,
    d_proj_ref,
    mixed_ref,
    grads_ref,
    d_bias_x_ref,
    normed_ref,
    inv_ref,
    w_qkvg_ref,
    gain_ref,
    restore_ref,
    d_wbias_ref,
    d_pair_hbm,
    d_qkvg_hbm,
    d_wout_hbm,
    d_wbias_hbm,
    d_gain_hbm,
    d_pair_ref,
    d_qkvg_ref,
    d_wout_ref,
    d_gain_ref,
    d_xn_ref,
    sems,
):
    me = lax.axis_index("row")
    chunk = grads_ref.shape[1]
    copies = [
        pltpu.make_async_copy(src, dst, sems.at[index])
        for index, (src, dst) in enumerate(
            (
                (d_wbias_ref, d_wbias_hbm),
                (d_qkvg_ref, d_qkvg_hbm),
                (d_wout_ref, d_wout_hbm),
                (d_gain_ref, d_gain_hbm),
                (d_pair_ref, d_pair_hbm),
            )
        )
    ]
    copies[0].start()
    d_proj = d_proj_ref[...]
    gain = gain_ref[...]
    d_qkvg_ref[...] = mm(tokens_ref[...], d_proj, (0, 0)) * inv_count
    copies[1].start()
    grads = grads_ref[...].reshape(mixed_ref.shape)
    d_wout_ref[...] = mm(mixed_ref[...], grads, (0, 0)) * inv_count
    copies[2].start()
    d_tokens = mm(d_proj, w_qkvg_ref[...], (1, 1)).astype(BF16)
    d_xn = mm(restore_ref[...], d_tokens) + d_bias_x_ref[...].astype(F32)
    d_xn_ref[...] = d_xn
    d_gain_ref[...] = jnp.sum(d_xn * normed_ref[...], axis=0, keepdims=True) * inv_count
    copies[3].start()
    own = pl.ds(pl.multiple_of(me * chunk, chunk), chunk)
    normed = normed_ref[own, :]
    scaled = d_xn_ref[own, :] * gain
    d_pair = inv_ref[own, :] * (
        scaled
        - jnp.mean(scaled, axis=-1, keepdims=True)
        - normed * jnp.mean(scaled * normed, axis=-1, keepdims=True)
    )
    d_pair_ref[...] = d_pair.astype(BF16).reshape(d_pair_ref.shape)
    copies[4].start()
    for copy in copies:
        copy.wait()


def gathered_plan(n, pair, out_grad, w_qkvg, w_out, w_bias, gain):
    local, length, width = pair.shape
    heads = w_bias.shape[1]
    cells = length * length
    chunk = local * length
    vmem = pl.BlockSpec(memory_space=pltpu.VMEM)
    hbm = pl.BlockSpec(memory_space=pltpu.HBM)
    shapes = [
        jax.ShapeDtypeStruct(pair.shape, BF16),
        jax.ShapeDtypeStruct(w_qkvg.shape, F32),
        jax.ShapeDtypeStruct(w_out.shape, F32),
        jax.ShapeDtypeStruct((heads, width), F32),
        jax.ShapeDtypeStruct((1, width), F32),
    ]
    operands = (
        pair.reshape(chunk, width),
        out_grad.reshape(chunk, width),
        w_qkvg,
        w_out,
        w_bias.T,
        gain.reshape(1, width),
    )
    passed = [
        pltpu.VMEM((cells, width), BF16),
        pltpu.VMEM((cells, w_qkvg.shape[1]), BF16),
        pltpu.VMEM((cells, width), BF16),
        pltpu.VMEM((n, chunk, width), BF16),
        pltpu.VMEM((cells, width), BF16),
        pltpu.VMEM((cells, width), F32),
        pltpu.VMEM((cells, width), F32),
        pltpu.VMEM(w_qkvg.shape, BF16),
        pltpu.VMEM((1, width), F32),
        pltpu.VMEM((cells, cells), BF16),
        pltpu.VMEM((heads, width), F32),
    ]
    halfway = pl.pallas_call(
        functools.partial(whole_crop, n, local),
        out_shape=passed,
        in_specs=[hbm] * len(operands),
        out_specs=[vmem] * len(passed),
        scratch_shapes=[
            pltpu.VMEM((n, chunk, width), BF16),
            pltpu.VMEM(w_out.shape, BF16),
            pltpu.VMEM((heads, width), BF16),
            pltpu.SemaphoreType.DMA((2, n)),
            pltpu.SemaphoreType.DMA((2, n)),
            pltpu.SemaphoreType.DMA((len(operands),)),
        ],
        compiler_params=pltpu.CompilerParams(
            collective_id=0, has_side_effects=True, vmem_limit_bytes=VMEM_LIMIT
        ),
    )(*[pltpu.with_memory_space_constraint(value, pltpu.HBM) for value in operands])
    results = pl.pallas_call(
        functools.partial(finish, 1.0 / length),
        out_shape=shapes,
        in_specs=[vmem] * len(passed),
        out_specs=[hbm] * len(shapes),
        scratch_shapes=[
            pltpu.VMEM(pair.shape, BF16),
            pltpu.VMEM(w_qkvg.shape, F32),
            pltpu.VMEM(w_out.shape, F32),
            pltpu.VMEM((1, width), F32),
            pltpu.VMEM((cells, width), F32),
            pltpu.SemaphoreType.DMA((len(shapes),)),
        ],
        compiler_params=pltpu.CompilerParams(vmem_limit_bytes=VMEM_LIMIT),
    )(*halfway)
    d_pair, d_qkvg, d_wout, d_wbias, d_gain = results
    return (d_pair, d_qkvg, d_wout, d_wbias.T, d_gain.reshape(width))


def per_device(n, pair, out_grad, w_qkvg, w_out, w_bias, gain):
    local, length, width = pair.shape
    chunk = local * length
    powers = all(size & (size - 1) == 0 for size in (n, local, length, width, w_bias.shape[1]))
    fits = n > 1 and width == BLOCK and chunk % 16 == 0 and BLOCK % chunk == 0
    if powers and fits and length * length % BLOCK == 0 and length <= 32:
        return gathered_plan(n, pair, out_grad, w_qkvg, w_out, w_bias, gain)
    return sharded_plan(pair, out_grad, w_qkvg, w_out, w_bias, gain)


def solution(mesh):
    in_specs = (P(("crop", "row"), None, None), P("crop", "row", None), P(), P(), P(), P())
    out_specs = (
        P(("crop", "row"), None, None),
        P("crop", None),
        P("crop", None),
        P("crop", None),
        P("crop"),
    )
    return jax.shard_map(
        functools.partial(per_device, mesh.shape["row"]),
        mesh=mesh,
        in_specs=in_specs, out_specs=out_specs, check_vma=False
    )
```

```python
import functools

import jax
import jax.numpy as jnp
from jax import lax
from jax.experimental import pallas as pl
from jax.experimental.pallas import tpu as pltpu
from jax.sharding import PartitionSpec as P

DH = 32


EPSILON = 1e-05


def normalize(pair, gain):
    values = pair.astype(jnp.float32)
    center = jnp.mean(values, axis=-1, keepdims=True)
    spread = jnp.mean(jnp.square(values - center), axis=-1, keepdims=True)
    inv_std = lax.rsqrt(spread + EPSILON)
    normed = (values - center) * inv_std
    return ((normed * gain).astype(jnp.bfloat16), normed, inv_std)


def column_grad(tokens, grads, w_qkvg, w_out, bias, scale):
    width = w_out.shape[0]
    heads = bias.shape[0]
    size = width // heads
    count = tokens.shape[0]
    proj = jnp.dot(tokens, w_qkvg, preferred_element_type=jnp.float32)
    queries = proj[:, :width].astype(jnp.bfloat16).reshape(count, heads, size)
    keys = proj[:, width : 2 * width].astype(jnp.bfloat16).reshape(count, heads, size)
    values = proj[:, 2 * width : 3 * width].astype(jnp.bfloat16).reshape(count, heads, size)
    gate = jax.nn.sigmoid(proj[:, 3 * width :]).reshape(count, heads, size)
    scores = jnp.einsum("khd,ihd->hki", keys, queries, preferred_element_type=jnp.float32) * scale
    scores = scores + bias.astype(jnp.float32)
    probs = jax.nn.softmax(scores, axis=1)
    probs_b = probs.astype(jnp.bfloat16)
    attended = jnp.einsum("hki,khd->ihd", probs_b, values, preferred_element_type=jnp.float32)
    mixed = (gate * attended).astype(jnp.bfloat16).reshape(count, width)
    d_mixed = lax.dot_general(
        grads, w_out, (((1,), (1,)), ((), ())), preferred_element_type=jnp.float32
    ).reshape(count, heads, size)
    part_wout = lax.dot_general(
        mixed, grads, (((0,), (0,)), ((), ())), preferred_element_type=jnp.float32
    )
    d_gate = d_mixed * attended * gate * (1.0 - gate)
    d_att = (d_mixed * gate).astype(jnp.bfloat16)
    d_values = jnp.einsum("hki,ihd->khd", probs_b, d_att, preferred_element_type=jnp.float32)
    d_probs = jnp.einsum("ihd,khd->hki", d_att, values, preferred_element_type=jnp.float32)
    delta = jnp.sum(d_att.astype(jnp.float32) * attended, axis=-1)
    d_scores = (probs * (d_probs - delta.T[:, None, :])).astype(jnp.bfloat16)
    d_queries = (
        jnp.einsum("hki,khd->ihd", d_scores, keys, preferred_element_type=jnp.float32) * scale
    )
    d_keys = (
        jnp.einsum("hki,ihd->khd", d_scores, queries, preferred_element_type=jnp.float32) * scale
    )
    d_proj = jnp.concatenate(
        [
            d_queries.reshape(count, width),
            d_keys.reshape(count, width),
            d_values.reshape(count, width),
            d_gate.reshape(count, width),
        ],
        axis=1,
    ).astype(jnp.bfloat16)
    part_qkvg = lax.dot_general(
        tokens, d_proj, (((0,), (0,)), ((), ())), preferred_element_type=jnp.float32
    )
    d_tokens = lax.dot_general(
        d_proj, w_qkvg, (((1,), (1,)), ((), ())), preferred_element_type=jnp.float32
    ).astype(jnp.bfloat16)
    return (d_tokens, d_scores, part_qkvg, part_wout, queries, keys, values, d_att, delta)


def sharded_plan(pair, out_grad, w_qkvg, w_out, w_bias, gain):
    normed_b, normed, inv_std = normalize(pair, gain)
    width = w_out.shape[0]
    heads = w_bias.shape[1]
    scale = DH ** (-0.5)
    columns = lax.all_to_all(normed_b, "row", split_axis=1, concat_axis=0, tiled=True)
    wide_bias = w_bias.astype(jnp.float32)
    local_bias = jnp.einsum(
        "abc,ch->hab", normed_b, w_bias, preferred_element_type=jnp.float32
    ).astype(jnp.bfloat16)
    bias = lax.all_gather(local_bias, "row", axis=1, tiled=True)
    length = bias.shape[1]
    inv_count = 1.0 / length
    inputs = (jnp.swapaxes(columns, 0, 1), jnp.swapaxes(out_grad, 0, 1))

    def step(carry, pieces):
        d_bias, d_qkvg, d_wout = carry
        outs = column_grad(pieces[0], pieces[1], w_qkvg, w_out, bias, scale)
        return ((d_bias + outs[1].astype(jnp.float32), d_qkvg + outs[2], d_wout + outs[3]), outs[0])

    start = (
        jnp.zeros((heads, length, length), jnp.float32),
        jnp.zeros((width, 4 * width), jnp.float32),
        jnp.zeros((width, width), jnp.float32),
    )
    (d_bias, d_qkvg, d_wout), d_cols = lax.scan(step, start, inputs)
    d_att_cols = jnp.swapaxes(d_cols, 0, 1)
    owned = lax.psum_scatter(d_bias, "row", scatter_dimension=1, tiled=True)
    d_att_x = lax.all_to_all(d_att_cols, "row", split_axis=0, concat_axis=1, tiled=True)
    d_bias_x = jnp.einsum("hab,ch->abc", owned, wide_bias, precision=lax.Precision.HIGHEST).astype(
        jnp.bfloat16
    )
    d_wbias = jnp.einsum(
        "abc,hab->ch", normed_b.astype(jnp.float32), owned, precision=lax.Precision.HIGHEST
    )
    d_xn = d_att_x.astype(jnp.float32) + d_bias_x.astype(jnp.float32)
    local_gain = jnp.sum(d_xn * normed, axis=(0, 1))
    scaled = d_xn * gain
    d_pair = (
        inv_std
        * (
            scaled
            - jnp.mean(scaled, axis=-1, keepdims=True)
            - normed * jnp.mean(scaled * normed, axis=-1, keepdims=True)
        )
    ).astype(jnp.bfloat16)
    total_qkvg, total_wout, total_wbias, total_gain = lax.psum(
        (d_qkvg, d_wout, d_wbias, local_gain), "row"
    )
    return (
        d_pair,
        total_qkvg * inv_count,
        total_wout * inv_count,
        total_wbias * inv_count,
        total_gain * inv_count,
    )


BLOCK = 128
VMEM_LIMIT = 16 * 1024 * 1024
MASKED = -1e30
BF16 = jnp.bfloat16
F32 = jnp.float32


def mm(a, b, dims=(1, 0)):
    return lax.dot_general(
        a, b, (((dims[0],), (dims[1],)), ((), ())), preferred_element_type=F32
    )


def log2(value):
    return value.bit_length() - 1


def whole_crop(
    n,
    local,
    pair_hbm,
    grad_hbm,
    w_qkvg_hbm,
    w_out_hbm,
    w_bias_hbm,
    gain_hbm,
    d_pair_ref,
    d_qkvg_ref,
    d_wout_ref,
    d_wbias_ref,
    d_gain_ref,
    pairs_ref,
    grads_ref,
    w_qkvg_ref,
    w_out_ref,
    w_bias_ref,
    gain_ref,
    d_xn_ref,
    normed_ref,
    inv_ref,
    send_sems,
    recv_sems,
    local_sems,
):
    me = lax.axis_index("row")
    loads = [
        pltpu.make_async_copy(src, dst, local_sems.at[index])
        for index, (src, dst) in enumerate(
            (
                (pair_hbm, pairs_ref.at[me]),
                (grad_hbm, grads_ref.at[me]),
                (gain_hbm, gain_ref),
                (w_qkvg_hbm, w_qkvg_ref),
                (w_bias_hbm, w_bias_ref),
                (w_out_hbm, w_out_ref),
            )
        )
    ]
    loads[0].start()
    loads[1].start()
    barrier = pltpu.get_barrier_semaphore()
    for offset in range(1, n):
        pl.semaphore_signal(
            barrier,
            inc=1,
            device_id={"row": lax.rem(me + offset, n)},
            device_id_type=pl.DeviceIdType.MESH,
        )
    pl.semaphore_wait(barrier, n - 1)
    sent = []
    for kind, blocks in enumerate((pairs_ref, grads_ref)):
        loads[kind].wait()
        for offset in range(1, n):
            copy = pltpu.make_async_remote_copy(
                src_ref=blocks.at[me],
                dst_ref=blocks.at[me],
                send_sem=send_sems.at[kind, offset],
                recv_sem=recv_sems.at[kind, offset],
                device_id={"row": lax.rem(me + offset, n)},
                device_id_type=pl.DeviceIdType.MESH,
            )
            copy.start()
            sent.append(copy)
        if kind == 0:
            for copy in loads[2:]:
                copy.start()

    chunk = pairs_ref.shape[1]
    width = pairs_ref.shape[2]
    heads = w_bias_ref.shape[0]
    size = width // heads
    length = chunk // local
    cells = length * length
    scale = size ** (-0.5)
    inv_count = 1.0 / length
    s_local, s_length, s_chunk = log2(local), log2(length), log2(chunk)

    def iota(shape, axis):
        return lax.broadcasted_iota(jnp.int32, shape, axis)

    def row_of(position):
        return (position & (chunk - 1)) >> s_local

    g, r = iota((cells, cells), 0), iota((cells, cells), 1)
    cell = (row_of(g) << s_length) + ((g >> s_chunk) << s_local) + (g & (local - 1))
    permute = (cell == r).astype(F32).astype(BF16)
    r, g = iota((cells, cells), 0), iota((cells, cells), 1)
    cell = (row_of(g) << s_length) + ((g >> s_chunk) << s_local) + (g & (local - 1))
    restore = (cell == r).astype(F32).astype(BF16)
    p, q = iota((BLOCK, BLOCK), 0), iota((BLOCK, BLOCK), 1)
    same_column = ((p >> s_chunk) == (q >> s_chunk)) & (((p ^ q) & (local - 1)) == 0)
    p, r = iota((BLOCK, cells), 0), iota((BLOCK, cells), 1)
    spread_key = (row_of(p) == (r >> s_length)).astype(F32).astype(BF16)
    r, p = iota((cells, BLOCK), 0), iota((cells, BLOCK), 1)
    pick_key = (row_of(p) == (r >> s_length)).astype(F32).astype(BF16)
    pick_query = row_of(p) == (r & (length - 1))
    lane_head = iota((BLOCK, width), 1) >> log2(size)

    def per_head(block):
        zero = jnp.zeros_like(block)
        return jnp.concatenate([jnp.where(lane_head == h, block, zero) for h in range(heads)], 0)

    def own_head(stacked):
        out = stacked[:BLOCK]
        for h in range(1, heads):
            out = jnp.where(lane_head == h, stacked[h * BLOCK : (h + 1) * BLOCK], out)
        return out

    for copy in loads[2:5]:
        copy.wait()
    for copy in sent[: n - 1]:
        copy.wait_recv()

    w_bias = w_bias_ref[...]
    w_bias_rows = jnp.concatenate(
        [jnp.broadcast_to(w_bias[h : h + 1], (BLOCK, width)) for h in range(heads)], 0
    ).astype(BF16)
    w_qkvg = w_qkvg_ref[...]
    gain = gain_ref[...]

    values = pairs_ref[...].reshape(cells, width).astype(F32)
    center = jnp.mean(values, axis=-1, keepdims=True)
    spread = jnp.mean(jnp.square(values - center), axis=-1, keepdims=True)
    inv_std = lax.rsqrt(spread + EPSILON)
    normed = (values - center) * inv_std
    xn = (normed * gain).astype(BF16)
    normed_ref[...] = normed
    inv_ref[...] = jnp.broadcast_to(inv_std, (cells, width))

    tokens = mm(permute, xn).astype(BF16)
    proj = mm(tokens, w_qkvg)
    bias_cells = mm(xn, w_bias_rows, (1, 1))
    bias = mm(
        spread_key,
        jnp.concatenate(
            [
                jnp.where(pick_query, bias_cells[:, h * BLOCK : (h + 1) * BLOCK], 0.0)
                for h in range(heads)
            ],
            1,
        ).astype(BF16),
    )
    bias = jnp.concatenate(
        [
            jnp.where(same_column, bias[:, h * BLOCK : (h + 1) * BLOCK], MASKED)
            for h in range(heads)
        ],
        0,
    )
    forward = []
    for start in range(0, cells, BLOCK):
        rows = slice(start, start + BLOCK)
        queries = proj[rows, :width].astype(BF16)
        keys = per_head(proj[rows, width : 2 * width]).astype(BF16)
        vals = per_head(proj[rows, 2 * width : 3 * width]).astype(BF16)
        gate = jax.nn.sigmoid(proj[rows, 3 * width :])
        scores = mm(keys, queries, (1, 1)) * scale + bias
        scores = scores.reshape(heads, BLOCK, BLOCK)
        top = jnp.max(scores, axis=1, keepdims=True)
        weights = jnp.exp(scores - top)
        probs = weights * (1.0 / jnp.sum(weights, axis=1, keepdims=True))
        probs_b = probs.astype(BF16)
        flat_b = probs_b.reshape(heads * BLOCK, BLOCK)
        attended = mm(flat_b, vals, (0, 0))
        forward.append((queries, keys, vals, gate, probs, probs_b, attended))

    for copy in loads[5:]:
        copy.wait()
    for copy in sent[n - 1 :]:
        copy.wait_recv()
    grads = grads_ref[...].reshape(cells, width)
    d_mixed_all = mm(grads, w_out_ref[...], (1, 1))

    mixed_parts, d_proj_parts = [], []
    d_bias_x = jnp.zeros((cells, width), F32)
    d_wbias = jnp.zeros((heads * BLOCK, width), F32)
    for start in range(0, cells, BLOCK):
        queries, keys, vals, gate, probs, probs_b, attended = forward[start // BLOCK]
        rows = slice(start, start + BLOCK)
        flat_b = probs_b.reshape(heads * BLOCK, BLOCK)
        d_mixed = d_mixed_all[rows]
        mixed_parts.append((gate * attended).astype(BF16))
        d_gate = d_mixed * attended * gate * (1.0 - gate)
        d_att = (d_mixed * gate).astype(BF16)
        d_values = own_head(mm(flat_b, d_att))
        d_probs = mm(vals, d_att, (1, 1)).reshape(heads, BLOCK, BLOCK)
        delta = jnp.sum(probs_b.astype(F32) * d_probs, axis=1, keepdims=True)
        d_scores = (probs * (d_probs - delta)).astype(BF16)
        flat_d = d_scores.reshape(heads * BLOCK, BLOCK)
        d_queries = mm(flat_d, keys, (0, 0)) * scale
        d_keys = own_head(mm(flat_d, queries)) * scale
        d_proj_parts.append(
            jnp.concatenate([d_queries, d_keys, d_values, d_gate], 1).astype(BF16)
        )
        terms = mm(pick_key, jnp.concatenate([d_scores[h] for h in range(heads)], 1))
        terms = jnp.concatenate(
            [
                jnp.where(pick_query, terms[:, h * BLOCK : (h + 1) * BLOCK], 0.0)
                for h in range(heads)
            ],
            1,
        ).astype(BF16)
        d_bias_x = d_bias_x + mm(terms, w_bias_rows)
        d_wbias = d_wbias + mm(terms, xn, (0, 0))

    d_proj = jnp.concatenate(d_proj_parts, 0)
    mixed = jnp.concatenate(mixed_parts, 0)
    d_qkvg_ref[...] = mm(tokens, d_proj, (0, 0)) * inv_count
    d_wout_ref[...] = mm(mixed, grads, (0, 0)) * inv_count
    d_wbias_ref[...] = jnp.sum(d_wbias.reshape(heads, BLOCK, width), axis=1) * inv_count
    d_tokens = mm(d_proj, w_qkvg, (1, 1)).astype(BF16)
    d_xn = mm(restore, d_tokens) + d_bias_x.astype(BF16).astype(F32)
    d_gain_ref[...] = jnp.sum(d_xn * normed, axis=0, keepdims=True) * inv_count
    d_xn_ref[...] = d_xn

    own = pl.ds(pl.multiple_of(me * chunk, chunk), chunk)
    normed = normed_ref[own, :]
    scaled = d_xn_ref[own, :] * gain
    d_pair = inv_ref[own, :] * (
        scaled
        - jnp.mean(scaled, axis=-1, keepdims=True)
        - normed * jnp.mean(scaled * normed, axis=-1, keepdims=True)
    )
    d_pair_ref[...] = d_pair.astype(BF16).reshape(d_pair_ref.shape)
    for copy in sent:
        copy.wait_send()


def deliver(count, *refs):
    copies = [
        pltpu.make_async_copy(refs[index], refs[count + index], refs[-1].at[index])
        for index in range(count)
    ]
    for copy in copies:
        copy.start()
    for copy in copies:
        copy.wait()


def gathered_plan(n, pair, out_grad, w_qkvg, w_out, w_bias, gain):
    local, length, width = pair.shape
    heads = w_bias.shape[1]
    cells = length * length
    chunk = local * length
    vmem = pl.BlockSpec(memory_space=pltpu.VMEM)
    hbm = pl.BlockSpec(memory_space=pltpu.HBM)
    shapes = [
        jax.ShapeDtypeStruct(pair.shape, BF16),
        jax.ShapeDtypeStruct(w_qkvg.shape, F32),
        jax.ShapeDtypeStruct(w_out.shape, F32),
        jax.ShapeDtypeStruct((heads, width), F32),
        jax.ShapeDtypeStruct((1, width), F32),
    ]
    operands = (
        pair.reshape(chunk, width),
        out_grad.reshape(chunk, width),
        w_qkvg,
        w_out,
        w_bias.T,
        gain.reshape(1, width),
    )
    results = pl.pallas_call(
        functools.partial(whole_crop, n, local),
        out_shape=[pltpu.VMEM(shape.shape, shape.dtype) for shape in shapes],
        in_specs=[hbm] * 6,
        out_specs=[vmem] * 5,
        scratch_shapes=[
            pltpu.VMEM((n, chunk, width), BF16),
            pltpu.VMEM((n, chunk, width), BF16),
            pltpu.VMEM(w_qkvg.shape, BF16),
            pltpu.VMEM(w_out.shape, BF16),
            pltpu.VMEM((heads, width), BF16),
            pltpu.VMEM((1, width), F32),
            pltpu.VMEM((cells, width), F32),
            pltpu.VMEM((cells, width), F32),
            pltpu.VMEM((cells, width), F32),
            pltpu.SemaphoreType.DMA((2, n)),
            pltpu.SemaphoreType.DMA((2, n)),
            pltpu.SemaphoreType.DMA((6,)),
        ],
        compiler_params=pltpu.CompilerParams(
            collective_id=0, has_side_effects=True, vmem_limit_bytes=VMEM_LIMIT
        ),
    )(*[pltpu.with_memory_space_constraint(value, pltpu.HBM) for value in operands])
    results = pl.pallas_call(
        functools.partial(deliver, len(shapes)),
        out_shape=shapes,
        in_specs=[vmem] * len(shapes),
        out_specs=[hbm] * len(shapes),
        scratch_shapes=[pltpu.SemaphoreType.DMA((len(shapes),))],
        compiler_params=pltpu.CompilerParams(vmem_limit_bytes=VMEM_LIMIT),
    )(*results)
    d_pair, d_qkvg, d_wout, d_wbias, d_gain = results
    return (d_pair, d_qkvg, d_wout, d_wbias.T, d_gain.reshape(width))


def per_device(n, pair, out_grad, w_qkvg, w_out, w_bias, gain):
    local, length, width = pair.shape
    chunk = local * length
    powers = all(size & (size - 1) == 0 for size in (local, length, width, w_bias.shape[1]))
    fits = n > 1 and width == BLOCK and chunk % 16 == 0 and BLOCK % chunk == 0
    if powers and fits and length * length % BLOCK == 0 and length <= 32:
        return gathered_plan(n, pair, out_grad, w_qkvg, w_out, w_bias, gain)
    return sharded_plan(pair, out_grad, w_qkvg, w_out, w_bias, gain)


def solution(mesh):
    in_specs = (P(("crop", "row"), None, None), P("crop", "row", None), P(), P(), P(), P())
    out_specs = (
        P(("crop", "row"), None, None),
        P("crop", None),
        P("crop", None),
        P("crop", None),
        P("crop"),
    )
    return jax.shard_map(
        functools.partial(per_device, mesh.shape["row"]),
        mesh=mesh,
        in_specs=in_specs, out_specs=out_specs, check_vma=False
    )
```

```python
import functools

import jax
import jax.numpy as jnp
from jax import lax
from jax.experimental import pallas as pl
from jax.experimental.pallas import tpu as pltpu
from jax.sharding import PartitionSpec as P

DH = 32


EPSILON = 1e-05


def normalize(pair, gain):
    values = pair.astype(jnp.float32)
    center = jnp.mean(values, axis=-1, keepdims=True)
    spread = jnp.mean(jnp.square(values - center), axis=-1, keepdims=True)
    inv_std = lax.rsqrt(spread + EPSILON)
    normed = (values - center) * inv_std
    return ((normed * gain).astype(jnp.bfloat16), normed, inv_std)


def column_grad(tokens, grads, w_qkvg, w_out, bias, scale):
    width = w_out.shape[0]
    heads = bias.shape[0]
    size = width // heads
    count = tokens.shape[0]
    proj = jnp.dot(tokens, w_qkvg, preferred_element_type=jnp.float32)
    queries = proj[:, :width].astype(jnp.bfloat16).reshape(count, heads, size)
    keys = proj[:, width : 2 * width].astype(jnp.bfloat16).reshape(count, heads, size)
    values = proj[:, 2 * width : 3 * width].astype(jnp.bfloat16).reshape(count, heads, size)
    gate = jax.nn.sigmoid(proj[:, 3 * width :]).reshape(count, heads, size)
    scores = jnp.einsum("khd,ihd->hki", keys, queries, preferred_element_type=jnp.float32) * scale
    scores = scores + bias.astype(jnp.float32)
    probs = jax.nn.softmax(scores, axis=1)
    probs_b = probs.astype(jnp.bfloat16)
    attended = jnp.einsum("hki,khd->ihd", probs_b, values, preferred_element_type=jnp.float32)
    mixed = (gate * attended).astype(jnp.bfloat16).reshape(count, width)
    d_mixed = lax.dot_general(
        grads, w_out, (((1,), (1,)), ((), ())), preferred_element_type=jnp.float32
    ).reshape(count, heads, size)
    part_wout = lax.dot_general(
        mixed, grads, (((0,), (0,)), ((), ())), preferred_element_type=jnp.float32
    )
    d_gate = d_mixed * attended * gate * (1.0 - gate)
    d_att = (d_mixed * gate).astype(jnp.bfloat16)
    d_values = jnp.einsum("hki,ihd->khd", probs_b, d_att, preferred_element_type=jnp.float32)
    d_probs = jnp.einsum("ihd,khd->hki", d_att, values, preferred_element_type=jnp.float32)
    delta = jnp.sum(d_att.astype(jnp.float32) * attended, axis=-1)
    d_scores = (probs * (d_probs - delta.T[:, None, :])).astype(jnp.bfloat16)
    d_queries = (
        jnp.einsum("hki,khd->ihd", d_scores, keys, preferred_element_type=jnp.float32) * scale
    )
    d_keys = (
        jnp.einsum("hki,ihd->khd", d_scores, queries, preferred_element_type=jnp.float32) * scale
    )
    d_proj = jnp.concatenate(
        [
            d_queries.reshape(count, width),
            d_keys.reshape(count, width),
            d_values.reshape(count, width),
            d_gate.reshape(count, width),
        ],
        axis=1,
    ).astype(jnp.bfloat16)
    part_qkvg = lax.dot_general(
        tokens, d_proj, (((0,), (0,)), ((), ())), preferred_element_type=jnp.float32
    )
    d_tokens = lax.dot_general(
        d_proj, w_qkvg, (((1,), (1,)), ((), ())), preferred_element_type=jnp.float32
    ).astype(jnp.bfloat16)
    return (d_tokens, d_scores, part_qkvg, part_wout, queries, keys, values, d_att, delta)


def sharded_plan(pair, out_grad, w_qkvg, w_out, w_bias, gain):
    normed_b, normed, inv_std = normalize(pair, gain)
    width = w_out.shape[0]
    heads = w_bias.shape[1]
    scale = DH ** (-0.5)
    columns = lax.all_to_all(normed_b, "row", split_axis=1, concat_axis=0, tiled=True)
    wide_bias = w_bias.astype(jnp.float32)
    local_bias = jnp.einsum(
        "abc,ch->hab", normed_b, w_bias, preferred_element_type=jnp.float32
    ).astype(jnp.bfloat16)
    bias = lax.all_gather(local_bias, "row", axis=1, tiled=True)
    length = bias.shape[1]
    inv_count = 1.0 / length
    inputs = (jnp.swapaxes(columns, 0, 1), jnp.swapaxes(out_grad, 0, 1))

    def step(carry, pieces):
        d_bias, d_qkvg, d_wout = carry
        outs = column_grad(pieces[0], pieces[1], w_qkvg, w_out, bias, scale)
        return ((d_bias + outs[1].astype(jnp.float32), d_qkvg + outs[2], d_wout + outs[3]), outs[0])

    start = (
        jnp.zeros((heads, length, length), jnp.float32),
        jnp.zeros((width, 4 * width), jnp.float32),
        jnp.zeros((width, width), jnp.float32),
    )
    (d_bias, d_qkvg, d_wout), d_cols = lax.scan(step, start, inputs)
    d_att_cols = jnp.swapaxes(d_cols, 0, 1)
    owned = lax.psum_scatter(d_bias, "row", scatter_dimension=1, tiled=True)
    d_att_x = lax.all_to_all(d_att_cols, "row", split_axis=0, concat_axis=1, tiled=True)
    d_bias_x = jnp.einsum("hab,ch->abc", owned, wide_bias, precision=lax.Precision.HIGHEST).astype(
        jnp.bfloat16
    )
    d_wbias = jnp.einsum(
        "abc,hab->ch", normed_b.astype(jnp.float32), owned, precision=lax.Precision.HIGHEST
    )
    d_xn = d_att_x.astype(jnp.float32) + d_bias_x.astype(jnp.float32)
    local_gain = jnp.sum(d_xn * normed, axis=(0, 1))
    scaled = d_xn * gain
    d_pair = (
        inv_std
        * (
            scaled
            - jnp.mean(scaled, axis=-1, keepdims=True)
            - normed * jnp.mean(scaled * normed, axis=-1, keepdims=True)
        )
    ).astype(jnp.bfloat16)
    total_qkvg, total_wout, total_wbias, total_gain = lax.psum(
        (d_qkvg, d_wout, d_wbias, local_gain), "row"
    )
    return (
        d_pair,
        total_qkvg * inv_count,
        total_wout * inv_count,
        total_wbias * inv_count,
        total_gain * inv_count,
    )


BLOCK = 128
VMEM_LIMIT = 16 * 1024 * 1024
MASKED = -1e30
BF16 = jnp.bfloat16
F32 = jnp.float32


def mm(a, b, dims=(1, 0)):
    return lax.dot_general(
        a, b, (((dims[0],), (dims[1],)), ((), ())), preferred_element_type=F32
    )


def log2(value):
    return value.bit_length() - 1


def whole_crop(
    n,
    local,
    pair_hbm,
    grad_hbm,
    w_qkvg_hbm,
    w_out_hbm,
    w_bias_hbm,
    gain_hbm,
    d_pair_ref,
    d_qkvg_ref,
    d_wout_ref,
    d_wbias_ref,
    d_gain_ref,
    pairs_ref,
    grads_ref,
    w_qkvg_ref,
    w_out_ref,
    w_bias_ref,
    gain_ref,
    d_xn_ref,
    normed_ref,
    inv_ref,
    send_sems,
    recv_sems,
    local_sems,
):
    me = lax.axis_index("row")
    loads = [
        pltpu.make_async_copy(src, dst, local_sems.at[index])
        for index, (src, dst) in enumerate(
            (
                (pair_hbm, pairs_ref.at[me]),
                (grad_hbm, grads_ref.at[me]),
                (gain_hbm, gain_ref),
                (w_qkvg_hbm, w_qkvg_ref),
                (w_bias_hbm, w_bias_ref),
                (w_out_hbm, w_out_ref),
            )
        )
    ]
    loads[0].start()
    loads[1].start()
    barrier = pltpu.get_barrier_semaphore()
    for offset in range(1, n):
        pl.semaphore_signal(
            barrier,
            inc=1,
            device_id={"row": lax.rem(me + offset, n)},
            device_id_type=pl.DeviceIdType.MESH,
        )
    pl.semaphore_wait(barrier, n - 1)
    sent = []
    for kind, blocks in enumerate((pairs_ref, grads_ref)):
        loads[kind].wait()
        for offset in sorted(range(1, n), key=lambda offset: min(offset, n - offset)):
            copy = pltpu.make_async_remote_copy(
                src_ref=blocks.at[me],
                dst_ref=blocks.at[me],
                send_sem=send_sems.at[kind, offset],
                recv_sem=recv_sems.at[kind, offset],
                device_id={"row": lax.rem(me + offset, n)},
                device_id_type=pl.DeviceIdType.MESH,
            )
            copy.start()
            sent.append(copy)
        if kind == 0:
            for copy in loads[2:]:
                copy.start()

    chunk = pairs_ref.shape[1]
    width = pairs_ref.shape[2]
    heads = w_bias_ref.shape[0]
    size = width // heads
    length = chunk // local
    cells = length * length
    scale = size ** (-0.5)
    inv_count = 1.0 / length
    s_local, s_length, s_chunk = log2(local), log2(length), log2(chunk)

    def iota(shape, axis):
        return lax.broadcasted_iota(jnp.int32, shape, axis)

    def row_of(position):
        return (position & (chunk - 1)) >> s_local

    g, r = iota((cells, cells), 0), iota((cells, cells), 1)
    cell = (row_of(g) << s_length) + ((g >> s_chunk) << s_local) + (g & (local - 1))
    permute = (cell == r).astype(F32).astype(BF16)
    r, g = iota((cells, cells), 0), iota((cells, cells), 1)
    cell = (row_of(g) << s_length) + ((g >> s_chunk) << s_local) + (g & (local - 1))
    restore = (cell == r).astype(F32).astype(BF16)
    p, q = iota((BLOCK, BLOCK), 0), iota((BLOCK, BLOCK), 1)
    same_column = ((p >> s_chunk) == (q >> s_chunk)) & (((p ^ q) & (local - 1)) == 0)
    p, r = iota((BLOCK, cells), 0), iota((BLOCK, cells), 1)
    spread_key = (row_of(p) == (r >> s_length)).astype(F32).astype(BF16)
    r, p = iota((cells, BLOCK), 0), iota((cells, BLOCK), 1)
    pick_key = (row_of(p) == (r >> s_length)).astype(F32).astype(BF16)
    pick_query = row_of(p) == (r & (length - 1))
    lane_head = iota((BLOCK, width), 1) >> log2(size)

    def per_head(block):
        zero = jnp.zeros_like(block)
        return jnp.concatenate([jnp.where(lane_head == h, block, zero) for h in range(heads)], 0)

    def own_head(stacked):
        out = stacked[:BLOCK]
        for h in range(1, heads):
            out = jnp.where(lane_head == h, stacked[h * BLOCK : (h + 1) * BLOCK], out)
        return out

    for copy in loads[2:5]:
        copy.wait()
    for copy in sent[: n - 1]:
        copy.wait_recv()

    w_bias = w_bias_ref[...]
    w_bias_rows = jnp.concatenate(
        [jnp.broadcast_to(w_bias[h : h + 1], (BLOCK, width)) for h in range(heads)], 0
    ).astype(BF16)
    w_qkvg = w_qkvg_ref[...]
    gain = gain_ref[...]

    values = pairs_ref[...].reshape(cells, width).astype(F32)
    center = jnp.mean(values, axis=-1, keepdims=True)
    spread = jnp.mean(jnp.square(values - center), axis=-1, keepdims=True)
    inv_std = lax.rsqrt(spread + EPSILON)
    normed = (values - center) * inv_std
    xn = (normed * gain).astype(BF16)
    normed_ref[...] = normed
    inv_ref[...] = jnp.broadcast_to(inv_std, (cells, width))

    tokens = mm(permute, xn).astype(BF16)
    proj = mm(tokens, w_qkvg)
    bias_cells = mm(xn, w_bias_rows, (1, 1))
    bias = mm(
        spread_key,
        jnp.concatenate(
            [
                jnp.where(pick_query, bias_cells[:, h * BLOCK : (h + 1) * BLOCK], 0.0)
                for h in range(heads)
            ],
            1,
        ).astype(BF16),
    )
    bias = jnp.concatenate(
        [
            jnp.where(same_column, bias[:, h * BLOCK : (h + 1) * BLOCK], MASKED)
            for h in range(heads)
        ],
        0,
    )
    forward = []
    for start in range(0, cells, BLOCK):
        rows = slice(start, start + BLOCK)
        queries = proj[rows, :width].astype(BF16)
        keys = per_head(proj[rows, width : 2 * width]).astype(BF16)
        vals = per_head(proj[rows, 2 * width : 3 * width]).astype(BF16)
        gate = jax.nn.sigmoid(proj[rows, 3 * width :])
        scores = mm(keys, queries, (1, 1)) * scale + bias
        scores = scores.reshape(heads, BLOCK, BLOCK)
        top = jnp.max(scores, axis=1, keepdims=True)
        weights = jnp.exp(scores - top)
        probs = weights * (1.0 / jnp.sum(weights, axis=1, keepdims=True))
        probs_b = probs.astype(BF16)
        flat_b = probs_b.reshape(heads * BLOCK, BLOCK)
        attended = mm(flat_b, vals, (0, 0))
        forward.append((queries, keys, vals, gate, probs, probs_b, attended))

    for copy in loads[5:]:
        copy.wait()
    for copy in sent[n - 1 :]:
        copy.wait_recv()
    grads = grads_ref[...].reshape(cells, width)
    d_mixed_all = mm(grads, w_out_ref[...], (1, 1))

    mixed_parts, d_proj_parts = [], []
    d_bias_x = jnp.zeros((cells, width), F32)
    d_wbias = jnp.zeros((heads * BLOCK, width), F32)
    for start in range(0, cells, BLOCK):
        queries, keys, vals, gate, probs, probs_b, attended = forward[start // BLOCK]
        rows = slice(start, start + BLOCK)
        flat_b = probs_b.reshape(heads * BLOCK, BLOCK)
        d_mixed = d_mixed_all[rows]
        mixed_parts.append((gate * attended).astype(BF16))
        d_gate = d_mixed * attended * gate * (1.0 - gate)
        d_att = (d_mixed * gate).astype(BF16)
        d_values = own_head(mm(flat_b, d_att))
        d_probs = mm(vals, d_att, (1, 1)).reshape(heads, BLOCK, BLOCK)
        delta = jnp.sum(probs_b.astype(F32) * d_probs, axis=1, keepdims=True)
        d_scores = (probs * (d_probs - delta)).astype(BF16)
        flat_d = d_scores.reshape(heads * BLOCK, BLOCK)
        d_queries = mm(flat_d, keys, (0, 0)) * scale
        d_keys = own_head(mm(flat_d, queries)) * scale
        d_proj_parts.append(
            jnp.concatenate([d_queries, d_keys, d_values, d_gate], 1).astype(BF16)
        )
        terms = mm(pick_key, jnp.concatenate([d_scores[h] for h in range(heads)], 1))
        terms = jnp.concatenate(
            [
                jnp.where(pick_query, terms[:, h * BLOCK : (h + 1) * BLOCK], 0.0)
                for h in range(heads)
            ],
            1,
        ).astype(BF16)
        d_bias_x = d_bias_x + mm(terms, w_bias_rows)
        d_wbias = d_wbias + mm(terms, xn, (0, 0))

    d_proj = jnp.concatenate(d_proj_parts, 0)
    mixed = jnp.concatenate(mixed_parts, 0)
    d_qkvg_ref[...] = mm(tokens, d_proj, (0, 0)) * inv_count
    d_wout_ref[...] = mm(mixed, grads, (0, 0)) * inv_count
    d_wbias_ref[...] = jnp.sum(d_wbias.reshape(heads, BLOCK, width), axis=1) * inv_count
    d_tokens = mm(d_proj, w_qkvg, (1, 1)).astype(BF16)
    d_xn = mm(restore, d_tokens) + d_bias_x.astype(BF16).astype(F32)
    d_gain_ref[...] = jnp.sum(d_xn * normed, axis=0, keepdims=True) * inv_count
    d_xn_ref[...] = d_xn

    own = pl.ds(pl.multiple_of(me * chunk, chunk), chunk)
    normed = normed_ref[own, :]
    scaled = d_xn_ref[own, :] * gain
    d_pair = inv_ref[own, :] * (
        scaled
        - jnp.mean(scaled, axis=-1, keepdims=True)
        - normed * jnp.mean(scaled * normed, axis=-1, keepdims=True)
    )
    d_pair_ref[...] = d_pair.astype(BF16).reshape(d_pair_ref.shape)
    for copy in sent:
        copy.wait_send()


def deliver(count, *refs):
    copies = [
        pltpu.make_async_copy(refs[index], refs[count + index], refs[-1].at[index])
        for index in range(count)
    ]
    for copy in copies:
        copy.start()
    for copy in copies:
        copy.wait()


def gathered_plan(n, pair, out_grad, w_qkvg, w_out, w_bias, gain):
    local, length, width = pair.shape
    heads = w_bias.shape[1]
    cells = length * length
    chunk = local * length
    vmem = pl.BlockSpec(memory_space=pltpu.VMEM)
    hbm = pl.BlockSpec(memory_space=pltpu.HBM)
    shapes = [
        jax.ShapeDtypeStruct(pair.shape, BF16),
        jax.ShapeDtypeStruct(w_qkvg.shape, F32),
        jax.ShapeDtypeStruct(w_out.shape, F32),
        jax.ShapeDtypeStruct((heads, width), F32),
        jax.ShapeDtypeStruct((1, width), F32),
    ]
    operands = (
        pair.reshape(chunk, width),
        out_grad.reshape(chunk, width),
        w_qkvg,
        w_out,
        w_bias.T,
        gain.reshape(1, width),
    )
    results = pl.pallas_call(
        functools.partial(whole_crop, n, local),
        out_shape=[pltpu.VMEM(shape.shape, shape.dtype) for shape in shapes],
        in_specs=[hbm] * 6,
        out_specs=[vmem] * 5,
        scratch_shapes=[
            pltpu.VMEM((n, chunk, width), BF16),
            pltpu.VMEM((n, chunk, width), BF16),
            pltpu.VMEM(w_qkvg.shape, BF16),
            pltpu.VMEM(w_out.shape, BF16),
            pltpu.VMEM((heads, width), BF16),
            pltpu.VMEM((1, width), F32),
            pltpu.VMEM((cells, width), F32),
            pltpu.VMEM((cells, width), F32),
            pltpu.VMEM((cells, width), F32),
            pltpu.SemaphoreType.DMA((2, n)),
            pltpu.SemaphoreType.DMA((2, n)),
            pltpu.SemaphoreType.DMA((6,)),
        ],
        compiler_params=pltpu.CompilerParams(
            collective_id=0, has_side_effects=True, vmem_limit_bytes=VMEM_LIMIT
        ),
    )(*[pltpu.with_memory_space_constraint(value, pltpu.HBM) for value in operands])
    results = pl.pallas_call(
        functools.partial(deliver, len(shapes)),
        out_shape=shapes,
        in_specs=[vmem] * len(shapes),
        out_specs=[hbm] * len(shapes),
        scratch_shapes=[pltpu.SemaphoreType.DMA((len(shapes),))],
        compiler_params=pltpu.CompilerParams(vmem_limit_bytes=VMEM_LIMIT),
    )(*results)
    d_pair, d_qkvg, d_wout, d_wbias, d_gain = results
    return (d_pair, d_qkvg, d_wout, d_wbias.T, d_gain.reshape(width))


def per_device(n, pair, out_grad, w_qkvg, w_out, w_bias, gain):
    local, length, width = pair.shape
    chunk = local * length
    powers = all(size & (size - 1) == 0 for size in (local, length, width, w_bias.shape[1]))
    fits = n > 1 and width == BLOCK and chunk % 16 == 0 and BLOCK % chunk == 0
    if powers and fits and length * length % BLOCK == 0 and length <= 32:
        return gathered_plan(n, pair, out_grad, w_qkvg, w_out, w_bias, gain)
    return sharded_plan(pair, out_grad, w_qkvg, w_out, w_bias, gain)


def solution(mesh):
    in_specs = (P(("crop", "row"), None, None), P("crop", "row", None), P(), P(), P(), P())
    out_specs = (
        P(("crop", "row"), None, None),
        P("crop", None),
        P("crop", None),
        P("crop", None),
        P("crop"),
    )
    return jax.shard_map(
        functools.partial(per_device, mesh.shape["row"]),
        mesh=mesh,
        in_specs=in_specs, out_specs=out_specs, check_vma=False
    )
```

```python
import functools

import jax
import jax.numpy as jnp
from jax import lax
from jax.experimental import pallas as pl
from jax.experimental.pallas import tpu as pltpu
from jax.sharding import PartitionSpec as P

DH = 32


EPSILON = 1e-05


def normalize(pair, gain):
    values = pair.astype(jnp.float32)
    center = jnp.mean(values, axis=-1, keepdims=True)
    spread = jnp.mean(jnp.square(values - center), axis=-1, keepdims=True)
    inv_std = lax.rsqrt(spread + EPSILON)
    normed = (values - center) * inv_std
    return ((normed * gain).astype(jnp.bfloat16), normed, inv_std)


def column_grad(tokens, grads, w_qkvg, w_out, bias, scale):
    width = w_out.shape[0]
    heads = bias.shape[0]
    size = width // heads
    count = tokens.shape[0]
    proj = jnp.dot(tokens, w_qkvg, preferred_element_type=jnp.float32)
    queries = proj[:, :width].astype(jnp.bfloat16).reshape(count, heads, size)
    keys = proj[:, width : 2 * width].astype(jnp.bfloat16).reshape(count, heads, size)
    values = proj[:, 2 * width : 3 * width].astype(jnp.bfloat16).reshape(count, heads, size)
    gate = jax.nn.sigmoid(proj[:, 3 * width :]).reshape(count, heads, size)
    scores = jnp.einsum("khd,ihd->hki", keys, queries, preferred_element_type=jnp.float32) * scale
    scores = scores + bias.astype(jnp.float32)
    probs = jax.nn.softmax(scores, axis=1)
    probs_b = probs.astype(jnp.bfloat16)
    attended = jnp.einsum("hki,khd->ihd", probs_b, values, preferred_element_type=jnp.float32)
    mixed = (gate * attended).astype(jnp.bfloat16).reshape(count, width)
    d_mixed = lax.dot_general(
        grads, w_out, (((1,), (1,)), ((), ())), preferred_element_type=jnp.float32
    ).reshape(count, heads, size)
    part_wout = lax.dot_general(
        mixed, grads, (((0,), (0,)), ((), ())), preferred_element_type=jnp.float32
    )
    d_gate = d_mixed * attended * gate * (1.0 - gate)
    d_att = (d_mixed * gate).astype(jnp.bfloat16)
    d_values = jnp.einsum("hki,ihd->khd", probs_b, d_att, preferred_element_type=jnp.float32)
    d_probs = jnp.einsum("ihd,khd->hki", d_att, values, preferred_element_type=jnp.float32)
    delta = jnp.sum(d_att.astype(jnp.float32) * attended, axis=-1)
    d_scores = (probs * (d_probs - delta.T[:, None, :])).astype(jnp.bfloat16)
    d_queries = (
        jnp.einsum("hki,khd->ihd", d_scores, keys, preferred_element_type=jnp.float32) * scale
    )
    d_keys = (
        jnp.einsum("hki,ihd->khd", d_scores, queries, preferred_element_type=jnp.float32) * scale
    )
    d_proj = jnp.concatenate(
        [
            d_queries.reshape(count, width),
            d_keys.reshape(count, width),
            d_values.reshape(count, width),
            d_gate.reshape(count, width),
        ],
        axis=1,
    ).astype(jnp.bfloat16)
    part_qkvg = lax.dot_general(
        tokens, d_proj, (((0,), (0,)), ((), ())), preferred_element_type=jnp.float32
    )
    d_tokens = lax.dot_general(
        d_proj, w_qkvg, (((1,), (1,)), ((), ())), preferred_element_type=jnp.float32
    ).astype(jnp.bfloat16)
    return (d_tokens, d_scores, part_qkvg, part_wout, queries, keys, values, d_att, delta)


def sharded_plan(pair, out_grad, w_qkvg, w_out, w_bias, gain):
    normed_b, normed, inv_std = normalize(pair, gain)
    width = w_out.shape[0]
    heads = w_bias.shape[1]
    scale = DH ** (-0.5)
    columns = lax.all_to_all(normed_b, "row", split_axis=1, concat_axis=0, tiled=True)
    wide_bias = w_bias.astype(jnp.float32)
    local_bias = jnp.einsum(
        "abc,ch->hab", normed_b, w_bias, preferred_element_type=jnp.float32
    ).astype(jnp.bfloat16)
    bias = lax.all_gather(local_bias, "row", axis=1, tiled=True)
    length = bias.shape[1]
    inv_count = 1.0 / length
    inputs = (jnp.swapaxes(columns, 0, 1), jnp.swapaxes(out_grad, 0, 1))

    def step(carry, pieces):
        d_bias, d_qkvg, d_wout = carry
        outs = column_grad(pieces[0], pieces[1], w_qkvg, w_out, bias, scale)
        return ((d_bias + outs[1].astype(jnp.float32), d_qkvg + outs[2], d_wout + outs[3]), outs[0])

    start = (
        jnp.zeros((heads, length, length), jnp.float32),
        jnp.zeros((width, 4 * width), jnp.float32),
        jnp.zeros((width, width), jnp.float32),
    )
    (d_bias, d_qkvg, d_wout), d_cols = lax.scan(step, start, inputs)
    d_att_cols = jnp.swapaxes(d_cols, 0, 1)
    owned = lax.psum_scatter(d_bias, "row", scatter_dimension=1, tiled=True)
    d_att_x = lax.all_to_all(d_att_cols, "row", split_axis=0, concat_axis=1, tiled=True)
    d_bias_x = jnp.einsum("hab,ch->abc", owned, wide_bias, precision=lax.Precision.HIGHEST).astype(
        jnp.bfloat16
    )
    d_wbias = jnp.einsum(
        "abc,hab->ch", normed_b.astype(jnp.float32), owned, precision=lax.Precision.HIGHEST
    )
    d_xn = d_att_x.astype(jnp.float32) + d_bias_x.astype(jnp.float32)
    local_gain = jnp.sum(d_xn * normed, axis=(0, 1))
    scaled = d_xn * gain
    d_pair = (
        inv_std
        * (
            scaled
            - jnp.mean(scaled, axis=-1, keepdims=True)
            - normed * jnp.mean(scaled * normed, axis=-1, keepdims=True)
        )
    ).astype(jnp.bfloat16)
    total_qkvg, total_wout, total_wbias, total_gain = lax.psum(
        (d_qkvg, d_wout, d_wbias, local_gain), "row"
    )
    return (
        d_pair,
        total_qkvg * inv_count,
        total_wout * inv_count,
        total_wbias * inv_count,
        total_gain * inv_count,
    )


BLOCK = 128
PIECE = 32
VMEM_LIMIT = 16 * 1024 * 1024
MASKED = -1e30
BF16 = jnp.bfloat16
F32 = jnp.float32


def mm(a, b, dims=(1, 0)):
    return lax.dot_general(
        a, b, (((dims[0],), (dims[1],)), ((), ())), preferred_element_type=F32
    )


def log2(value):
    return value.bit_length() - 1


def whole_crop(
    n,
    local,
    pair_hbm,
    grad_hbm,
    w_qkvg_hbm,
    w_out_hbm,
    w_bias_hbm,
    gain_hbm,
    d_pair_ref,
    d_qkvg_ref,
    d_wout_ref,
    d_wbias_ref,
    d_gain_ref,
    pairs_ref,
    grads_ref,
    w_qkvg_ref,
    w_out_ref,
    w_bias_ref,
    gain_ref,
    d_xn_ref,
    normed_ref,
    inv_ref,
    send_sems,
    recv_sems,
    local_sems,
):
    me = lax.axis_index("row")
    loads = [
        pltpu.make_async_copy(src, dst, local_sems.at[index])
        for index, (src, dst) in enumerate(
            (
                (pair_hbm, pairs_ref.at[me]),
                (grad_hbm, grads_ref.at[me]),
                (gain_hbm, gain_ref),
                (w_qkvg_hbm, w_qkvg_ref),
                (w_bias_hbm, w_bias_ref),
                (w_out_hbm, w_out_ref),
            )
        )
    ]
    loads[0].start()
    loads[1].start()
    barrier = pltpu.get_barrier_semaphore()
    for offset in range(1, n):
        pl.semaphore_signal(
            barrier,
            inc=1,
            device_id={"row": lax.rem(me + offset, n)},
            device_id_type=pl.DeviceIdType.MESH,
        )
    pl.semaphore_wait(barrier, n - 1)
    sent = []
    for kind, blocks in enumerate((pairs_ref, grads_ref)):
        loads[kind].wait()
        for offset in range(1, n):
            copy = pltpu.make_async_remote_copy(
                src_ref=blocks.at[me],
                dst_ref=blocks.at[me],
                send_sem=send_sems.at[kind, offset],
                recv_sem=recv_sems.at[kind, offset],
                device_id={"row": lax.rem(me + offset, n)},
                device_id_type=pl.DeviceIdType.MESH,
            )
            copy.start()
            sent.append(copy)
        if kind == 0:
            for copy in loads[2:]:
                copy.start()

    chunk = pairs_ref.shape[1]
    width = pairs_ref.shape[2]
    heads = w_bias_ref.shape[0]
    size = width // heads
    length = chunk // local
    cells = length * length
    scale = size ** (-0.5)
    inv_count = 1.0 / length
    s_local, s_length, s_chunk = log2(local), log2(length), log2(chunk)

    def iota(shape, axis):
        return lax.broadcasted_iota(jnp.int32, shape, axis)

    def row_of(position):
        return (position & (chunk - 1)) >> s_local

    g, r = iota((cells, cells), 0), iota((cells, cells), 1)
    cell = (row_of(g) << s_length) + ((g >> s_chunk) << s_local) + (g & (local - 1))
    permute = (cell == r).astype(F32).astype(BF16)
    r, g = iota((cells, cells), 0), iota((cells, cells), 1)
    cell = (row_of(g) << s_length) + ((g >> s_chunk) << s_local) + (g & (local - 1))
    restore = (cell == r).astype(F32).astype(BF16)
    p, q = iota((BLOCK, BLOCK), 0), iota((BLOCK, BLOCK), 1)
    same_column = ((p >> s_chunk) == (q >> s_chunk)) & (((p ^ q) & (local - 1)) == 0)
    p, r = iota((BLOCK, cells), 0), iota((BLOCK, cells), 1)
    spread_key = (row_of(p) == (r >> s_length)).astype(F32).astype(BF16)
    r, p = iota((cells, BLOCK), 0), iota((cells, BLOCK), 1)
    pick_key = (row_of(p) == (r >> s_length)).astype(F32).astype(BF16)
    pick_query = row_of(p) == (r & (length - 1))
    lane_head = iota((BLOCK, width), 1) >> log2(size)

    def per_head(block):
        zero = jnp.zeros_like(block)
        return jnp.concatenate([jnp.where(lane_head == h, block, zero) for h in range(heads)], 0)

    def own_head(stacked):
        out = stacked[:BLOCK]
        for h in range(1, heads):
            out = jnp.where(lane_head == h, stacked[h * BLOCK : (h + 1) * BLOCK], out)
        return out

    for copy in loads[2:5]:
        copy.wait()
    for copy in sent[: n - 1]:
        copy.wait_recv()

    w_bias = w_bias_ref[...]
    w_bias_rows = jnp.concatenate(
        [jnp.broadcast_to(w_bias[h : h + 1], (BLOCK, width)) for h in range(heads)], 0
    ).astype(BF16)
    w_qkvg = w_qkvg_ref[...]
    gain = gain_ref[...]

    values = pairs_ref[...].reshape(cells, width).astype(F32)
    center = jnp.mean(values, axis=-1, keepdims=True)
    spread = jnp.mean(jnp.square(values - center), axis=-1, keepdims=True)
    inv_std = lax.rsqrt(spread + EPSILON)
    normed = (values - center) * inv_std
    xn = (normed * gain).astype(BF16)
    normed_ref[...] = normed
    inv_ref[...] = jnp.broadcast_to(inv_std, (cells, width))

    tokens = mm(permute, xn).astype(BF16)
    proj = mm(tokens, w_qkvg)
    bias_cells = mm(xn, w_bias_rows, (1, 1))
    bias = mm(
        spread_key,
        jnp.concatenate(
            [
                jnp.where(pick_query, bias_cells[:, h * BLOCK : (h + 1) * BLOCK], 0.0)
                for h in range(heads)
            ],
            1,
        ).astype(BF16),
    )
    bias = jnp.concatenate(
        [
            jnp.where(same_column, bias[:, h * BLOCK : (h + 1) * BLOCK], MASKED)
            for h in range(heads)
        ],
        0,
    )
    forward = []
    for start in range(0, cells, BLOCK):
        rows = slice(start, start + BLOCK)
        queries = proj[rows, :width].astype(BF16)
        keys = per_head(proj[rows, width : 2 * width]).astype(BF16)
        vals = per_head(proj[rows, 2 * width : 3 * width]).astype(BF16)
        gate = jax.nn.sigmoid(proj[rows, 3 * width :])
        scores = mm(keys, queries, (1, 1)) * scale + bias
        scores = scores.reshape(heads, BLOCK, BLOCK)
        top = jnp.max(scores, axis=1, keepdims=True)
        weights = jnp.exp(scores - top)
        probs = weights * (1.0 / jnp.sum(weights, axis=1, keepdims=True))
        probs_b = probs.astype(BF16)
        flat_b = probs_b.reshape(heads * BLOCK, BLOCK)
        attended = mm(flat_b, vals, (0, 0))
        forward.append((queries, keys, vals, gate, probs, probs_b, attended))

    for copy in loads[5:]:
        copy.wait()
    for copy in sent[n - 1 :]:
        copy.wait_recv()
    grads = grads_ref[...].reshape(cells, width)
    d_mixed_all = mm(grads, w_out_ref[...], (1, 1))

    mixed_parts, d_proj_parts = [], []
    d_bias_x = jnp.zeros((cells, width), F32)
    d_wbias = jnp.zeros((heads * BLOCK, width), F32)
    for start in range(0, cells, BLOCK):
        queries, keys, vals, gate, probs, probs_b, attended = forward[start // BLOCK]
        rows = slice(start, start + BLOCK)
        flat_b = probs_b.reshape(heads * BLOCK, BLOCK)
        d_mixed = d_mixed_all[rows]
        mixed_parts.append((gate * attended).astype(BF16))
        d_gate = d_mixed * attended * gate * (1.0 - gate)
        d_att = (d_mixed * gate).astype(BF16)
        d_values = own_head(mm(flat_b, d_att))
        d_probs = mm(vals, d_att, (1, 1)).reshape(heads, BLOCK, BLOCK)
        delta = jnp.sum(probs_b.astype(F32) * d_probs, axis=1, keepdims=True)
        d_scores = (probs * (d_probs - delta)).astype(BF16)
        flat_d = d_scores.reshape(heads * BLOCK, BLOCK)
        d_queries = mm(flat_d, keys, (0, 0)) * scale
        d_keys = own_head(mm(flat_d, queries)) * scale
        d_proj_parts.append(
            jnp.concatenate([d_queries, d_keys, d_values, d_gate], 1).astype(BF16)
        )
        terms = mm(pick_key, jnp.concatenate([d_scores[h] for h in range(heads)], 1))
        terms = jnp.concatenate(
            [
                jnp.where(pick_query, terms[:, h * BLOCK : (h + 1) * BLOCK], 0.0)
                for h in range(heads)
            ],
            1,
        ).astype(BF16)
        d_bias_x = d_bias_x + mm(terms, w_bias_rows)
        d_wbias = d_wbias + mm(terms, xn, (0, 0))

    d_proj = jnp.concatenate(d_proj_parts, 0)
    mixed = jnp.concatenate(mixed_parts, 0)
    d_qkvg_ref[...] = mm(tokens, d_proj, (0, 0)) * inv_count
    d_wout_ref[...] = mm(mixed, grads, (0, 0)) * inv_count
    d_wbias_ref[...] = jnp.sum(d_wbias.reshape(heads, BLOCK, width), axis=1) * inv_count
    d_tokens = mm(d_proj, w_qkvg, (1, 1)).astype(BF16)
    d_xn = mm(restore, d_tokens) + d_bias_x.astype(BF16).astype(F32)
    d_gain_ref[...] = jnp.sum(d_xn * normed, axis=0, keepdims=True) * inv_count
    d_xn_ref[...] = d_xn

    own = pl.ds(pl.multiple_of(me * chunk, chunk), chunk)
    normed = normed_ref[own, :]
    scaled = d_xn_ref[own, :] * gain
    d_pair = inv_ref[own, :] * (
        scaled
        - jnp.mean(scaled, axis=-1, keepdims=True)
        - normed * jnp.mean(scaled * normed, axis=-1, keepdims=True)
    )
    d_pair_ref[...] = d_pair.astype(BF16).reshape(d_pair_ref.shape)
    for copy in sent:
        copy.wait_send()


def deliver(count, *refs):
    pieces = []
    for index in range(count):
        rows = refs[index].shape[0]
        step = min(rows, PIECE)
        pieces += [(index, pl.ds(start, step)) for start in range(0, rows, step)]
    copies = [
        pltpu.make_async_copy(
            refs[index].at[rows], refs[count + index].at[rows], refs[-1].at[piece]
        )
        for piece, (index, rows) in enumerate(pieces)
    ]
    for copy in copies:
        copy.start()
    for copy in copies:
        copy.wait()


def gathered_plan(n, pair, out_grad, w_qkvg, w_out, w_bias, gain):
    local, length, width = pair.shape
    heads = w_bias.shape[1]
    cells = length * length
    chunk = local * length
    vmem = pl.BlockSpec(memory_space=pltpu.VMEM)
    hbm = pl.BlockSpec(memory_space=pltpu.HBM)
    shapes = [
        jax.ShapeDtypeStruct(pair.shape, BF16),
        jax.ShapeDtypeStruct(w_qkvg.shape, F32),
        jax.ShapeDtypeStruct(w_out.shape, F32),
        jax.ShapeDtypeStruct((heads, width), F32),
        jax.ShapeDtypeStruct((1, width), F32),
    ]
    operands = (
        pair.reshape(chunk, width),
        out_grad.reshape(chunk, width),
        w_qkvg,
        w_out,
        w_bias.T,
        gain.reshape(1, width),
    )
    results = pl.pallas_call(
        functools.partial(whole_crop, n, local),
        out_shape=[pltpu.VMEM(shape.shape, shape.dtype) for shape in shapes],
        in_specs=[hbm] * 6,
        out_specs=[vmem] * 5,
        scratch_shapes=[
            pltpu.VMEM((n, chunk, width), BF16),
            pltpu.VMEM((n, chunk, width), BF16),
            pltpu.VMEM(w_qkvg.shape, BF16),
            pltpu.VMEM(w_out.shape, BF16),
            pltpu.VMEM((heads, width), BF16),
            pltpu.VMEM((1, width), F32),
            pltpu.VMEM((cells, width), F32),
            pltpu.VMEM((cells, width), F32),
            pltpu.VMEM((cells, width), F32),
            pltpu.SemaphoreType.DMA((2, n)),
            pltpu.SemaphoreType.DMA((2, n)),
            pltpu.SemaphoreType.DMA((6,)),
        ],
        compiler_params=pltpu.CompilerParams(
            collective_id=0, has_side_effects=True, vmem_limit_bytes=VMEM_LIMIT
        ),
    )(*[pltpu.with_memory_space_constraint(value, pltpu.HBM) for value in operands])
    pieces = sum(-(-shape.shape[0] // PIECE) for shape in shapes)
    results = pl.pallas_call(
        functools.partial(deliver, len(shapes)),
        out_shape=shapes,
        in_specs=[vmem] * len(shapes),
        out_specs=[hbm] * len(shapes),
        scratch_shapes=[pltpu.SemaphoreType.DMA((pieces,))],
        compiler_params=pltpu.CompilerParams(vmem_limit_bytes=VMEM_LIMIT),
    )(*results)
    d_pair, d_qkvg, d_wout, d_wbias, d_gain = results
    return (d_pair, d_qkvg, d_wout, d_wbias.T, d_gain.reshape(width))


def per_device(n, pair, out_grad, w_qkvg, w_out, w_bias, gain):
    local, length, width = pair.shape
    chunk = local * length
    powers = all(size & (size - 1) == 0 for size in (local, length, width, w_bias.shape[1]))
    fits = n > 1 and width == BLOCK and chunk % 16 == 0 and BLOCK % chunk == 0
    if powers and fits and length * length % BLOCK == 0 and length <= 32:
        return gathered_plan(n, pair, out_grad, w_qkvg, w_out, w_bias, gain)
    return sharded_plan(pair, out_grad, w_qkvg, w_out, w_bias, gain)


def solution(mesh):
    in_specs = (P(("crop", "row"), None, None), P("crop", "row", None), P(), P(), P(), P())
    out_specs = (
        P(("crop", "row"), None, None),
        P("crop", None),
        P("crop", None),
        P("crop", None),
        P("crop"),
    )
    return jax.shard_map(
        functools.partial(per_device, mesh.shape["row"]),
        mesh=mesh,
        in_specs=in_specs, out_specs=out_specs, check_vma=False
    )
```
